32 devices in a mesh: res: 2 (over core), dp: 8 (over z, x), fsdp: 2 (over y).
Axes of the slice: x: 2, y: 2, z: 4, core: 2. Of those that a mesh axis runs over, the one named last changes fastest.
Arguments:
- tokens_in: bfloat16 [8192, 1024], P(('res', 'dp', 'fsdp')), may hold values from -6 to 6
- cotangent: bfloat16 [8192, 1024], P(('res', 'dp', 'fsdp')), may hold values from -6 to 6
- crop_counts: int32 [2, 8, 2, 2], P('res', 'dp', 'fsdp'), may hold values from 0 to 20, as said below
- group_tokens: int32 [2], replicated, may hold values from 1024 to 8191
- weight_qkv: float32 [1024, 3072], P('fsdp')
- rows_qkv: float32 [1024], P('fsdp'), may hold values from 655.36 to 5242.88
- cols_qkv: float32 [3072], replicated, may hold values from 655.36 to 5242.88
- weight_out: float32 [1024, 1024], P('fsdp')
- rows_out: float32 [1024], P('fsdp'), may hold values from 81.92 to 655.36
- cols_out: float32 [1024], replicated, may hold values from 81.92 to 655.36
- weight_up: float32 [1024, 4096], P('fsdp')
- rows_up: float32 [1024], P('fsdp'), may hold values from 81.92 to 655.36
- cols_up: float32 [4096], replicated, may hold values from 81.92 to 655.36
- weight_down: float32 [4096, 1024], P('fsdp')
- rows_down: float32 [4096], P('fsdp'), may hold values from 204.8 to 1638.4
- cols_down: float32 [1024], replicated, may hold values from 204.8 to 1638.4
- vectors: float32 [1024, 12], P('fsdp')
- moment_vec: float32 [1024, 12], P('fsdp'), may hold values from 204.8 to 1638.4
Outputs:
- tokens_out: bfloat16 [8192, 1024], P(('res', 'dp', 'fsdp'))
- grad_in: float32 [8192, 1024], P(('res', 'dp', 'fsdp'))
- grad_qkv: float32 [1024, 3072], P('fsdp')
- rows_qkv_new: float32 [1024], P('fsdp')
- cols_qkv_new: float32 [3072], replicated
- weight_qkv_new: float32 [1024, 3072], P('fsdp')
- weight_qkv_half: bfloat16 [1024, 3072], P('fsdp')
- grad_out: float32 [1024, 1024], P('fsdp')
- rows_out_new: float32 [1024], P('fsdp')
- cols_out_new: float32 [1024], replicated
- weight_out_new: float32 [1024, 1024], P('fsdp')
- weight_out_half: bfloat16 [1024, 1024], P('fsdp')
- grad_up: float32 [1024, 4096], P('fsdp')
- rows_up_new: float32 [1024], P('fsdp')
- cols_up_new: float32 [4096], replicated
- weight_up_new: float32 [1024, 4096], P('fsdp')
- weight_up_half: bfloat16 [1024, 4096], P('fsdp')
- grad_down: float32 [4096, 1024], P('fsdp')
- rows_down_new: float32 [4096], P('fsdp')
- cols_down_new: float32 [1024], replicated
- weight_down_new: float32 [4096, 1024], P('fsdp')
- weight_down_half: bfloat16 [4096, 1024], P('fsdp')
- grad_vectors: float32 [1024, 12], P('fsdp')
- moment_vec_new: float32 [1024, 12], P('fsdp')
- vectors_new: float32 [1024, 12], P('fsdp')
- vectors_half: bfloat16 [1024, 12], P('fsdp')
The draws below stay inside these ranges and needn't reach their ends.
Inputs may be any that keep to these rules, and one draw needn't show every extreme that they name: `crop_counts`: per device, entry 0 counts crops of 50 tokens (res group 0) or of 145 tokens (res group 1) and is 1 or more; entry 1 counts crops of 10 tokens in group 0 and is 0 in group 1. Crops fill the device's rows from the first one on, longer kind first, and fit in its 256 rows; the rows after them are padding.
All inputs are finite; a program needn't handle non-finite values.
Results may differ from the reference program's by a relative error of at most 0.014.
The reference program's roundings to bfloat16 on the way count: a program that leaves them out, or rounds other values in their place, can miss the bound.
Values may be sent and summed in bfloat16 or wider, within the bound.
No kernel may reach another device: no remote copies, remote signals or barrier semaphores. Data moves between devices by JAX's collectives and lax.ppermute only.
A program may use at most 320 MiB of HBM per device.

```python
import math
import jax
import jax.numpy as jnp
from jax import lax

D = 1024
HEADS = 16
HEAD = 64
FF = 4096
TOK_DEV = 256
GLOBAL_LEN = 50
LOCAL_LEN = 10
IMAGE_LEN = 145
STEP = 3
NVEC = 12
TOKENS = 8192
N_DP = 8
N_FSDP = 2


def rising(count, low_end, high_end):
    place = jnp.arange(count, dtype=jnp.float32) / max(count - 1, 1)
    return jnp.exp(jnp.log(jnp.float32(low_end)) + jnp.log(jnp.float32(high_end / low_end)) * place)


def draw_crop_counts(key, part):
    key = jax.random.fold_in(key, 11)
    keys = jax.random.split(key, 3)
    cells = N_DP * N_FSDP
    most_global = TOK_DEV // GLOBAL_LEN
    global_count = jax.random.randint(keys[0], (cells,), 1, most_global + 1)
    global_count = global_count.at[0].set(most_global).at[cells - 1].set(1)
    room = (TOK_DEV - GLOBAL_LEN * global_count) // LOCAL_LEN
    local_count = jax.random.randint(keys[1], (cells,), 0, room + 1)
    local_count = local_count.at[cells - 1].set(room[cells - 1])
    most_image = TOK_DEV // IMAGE_LEN
    image_count = jax.random.randint(keys[2], (cells,), 1, most_image + 1)
    image_count = image_count.at[0].set(most_image)
    first = jnp.stack([global_count, local_count], axis=-1)
    second = jnp.stack([image_count, jnp.zeros_like(image_count)], axis=-1)
    return jnp.stack([first, second]).reshape(2, N_DP, N_FSDP, 2).astype(jnp.int32)


def draw_weight_qkv(key, part):
    key = jax.random.fold_in(key, 21)
    noise = jax.random.normal(key, (D, 3 * D), jnp.float32)
    columns = jnp.tile(rising(D, 0.6, 1.8), 3)
    return noise * D ** (-0.5) * rising(D, 0.6, 1.8)[:, None] * columns[None, :]


def draw_weight_out(key, part):
    key = jax.random.fold_in(key, 22)
    noise = jax.random.normal(key, (D, D), jnp.float32)
    return noise * 4.0 * D ** (-0.5) * rising(D, 0.6, 1.8)[:, None]


def draw_weight_up(key, part):
    key = jax.random.fold_in(key, 23)
    noise = jax.random.normal(key, (D, FF), jnp.float32)
    return noise * D ** (-0.5) * rising(D, 0.6, 1.8)[:, None] * rising(FF, 0.6, 1.8)[None, :]


def draw_weight_down(key, part):
    key = jax.random.fold_in(key, 24)
    noise = jax.random.normal(key, (FF, D), jnp.float32)
    return noise * FF ** (-0.5) * rising(FF, 0.6, 1.8)[:, None]


def draw_vectors(key, part):
    key = jax.random.fold_in(key, 25)
    keys = jax.random.split(key, 2)
    noise = jax.random.normal(keys[0], (D, NVEC), jnp.float32)
    jitter = jax.random.uniform(keys[1], (D, NVEC), jnp.float32, 0.85, 1.15)
    column = jnp.arange(NVEC)[None, :]
    gain_column = (column == NVEC - 4) | (column == NVEC - 2)
    gains = rising(D, 0.6, 1.8)[:, None] * jitter
    return jnp.where(gain_column, gains, 0.3 * noise)


def block_scale(key, shape, cuts, least, top_value):
    def one(axis_at, blocks):
        draws = jax.random.uniform(jax.random.fold_in(jax.random.fold_in(key, 6), axis_at), (blocks,), jnp.float32, least / len(cuts), top_value / len(cuts))
        return jnp.repeat(jnp.exp(draws), shape[axis_at] // blocks).reshape((-1,) + (1,) * (len(shape) - axis_at - 1))

    level = one(*cuts[0])
    for cut in cuts[1:]:
        level = level * one(*cut)
    return level


def scatter_about(rng, dims, deviation, most, cuts=(), held_as=jnp.bfloat16):
    loudness = block_scale(rng, dims, cuts, -0.22, 0.18) if cuts else 1.0
    array = jax.random.normal(rng, dims, jnp.float32) * deviation * loudness
    return jnp.minimum(jnp.maximum(array, -most), most).astype(held_as)


def setup_inputs(seed: int = 0) -> dict:
    streams_of = jax.random.split(jax.random.key(seed), 19)
    tokens_in = scatter_about(streams_of[0], (TOKENS, D), 1.0, 6.0, ((0, 32),))
    cotangent = scatter_about(streams_of[1], (TOKENS, D), 1.0, 6.0, ((0, 32),))
    crop_counts = draw_crop_counts(jax.random.fold_in(streams_of[18], 71), 0)
    group_tokens = jax.random.randint(streams_of[3], (2,), 1024, 8192).astype(jnp.int32)
    weight_qkv = draw_weight_qkv(jax.random.fold_in(streams_of[18], 71), 0)
    rows_qkv = jnp.clip(jnp.exp(math.log(5242.88) - 2.0794415 * jax.random.uniform(streams_of[5], (D,), jnp.float32) ** block_scale(streams_of[5], (D,), ((0, 2),), -0.2, 0.2)), 655.36, 5242.88)
    cols_qkv = jnp.clip(jnp.exp(jax.random.uniform(streams_of[6], (3 * D,), jnp.float32, math.log(655.36), math.log(5242.88))), 655.36, 5242.88)
    weight_out = draw_weight_out(jax.random.fold_in(streams_of[18], 71), 0)
    rows_out = jnp.clip(jnp.exp(math.log(655.36) - 2.0794415 * jax.random.uniform(streams_of[8], (D,), jnp.float32) ** block_scale(streams_of[8], (D,), ((0, 2),), -0.2, 0.2)), 81.92, 655.36)
    cols_out = jnp.clip(jnp.exp(jax.random.uniform(streams_of[9], (D,), jnp.float32, math.log(81.92), math.log(655.36))), 81.92, 655.36)
    weight_up = draw_weight_up(jax.random.fold_in(streams_of[18], 71), 0)
    rows_up = jnp.clip(jnp.exp(math.log(655.36) - 2.0794415 * jax.random.uniform(streams_of[11], (D,), jnp.float32) ** block_scale(streams_of[11], (D,), ((0, 2),), -0.2, 0.2)), 81.92, 655.36)
    cols_up = jnp.clip(jnp.exp(jax.random.uniform(streams_of[12], (FF,), jnp.float32, math.log(81.92), math.log(655.36))), 81.92, 655.36)
    weight_down = draw_weight_down(jax.random.fold_in(streams_of[18], 71), 0)
    rows_down = jnp.clip(jnp.exp(math.log(1638.4) - 2.0794415 * jax.random.uniform(streams_of[14], (FF,), jnp.float32) ** block_scale(streams_of[14], (FF,), ((0, 2),), -0.2, 0.2)), 204.8, 1638.4)
    cols_down = jnp.clip(jnp.exp(jax.random.uniform(streams_of[15], (D,), jnp.float32, math.log(204.8), math.log(1638.4))), 204.8, 1638.4)
    vectors = draw_vectors(jax.random.fold_in(streams_of[18], 71), 0)
    moment_vec = jnp.clip(jnp.exp(math.log(1638.4) - 2.0794415 * jax.random.uniform(streams_of[17], (D, NVEC), jnp.float32) ** block_scale(streams_of[17], (D, NVEC), ((0, 2),), -0.2, 0.2)), 204.8, 1638.4)
    return {"tokens_in": tokens_in, "cotangent": cotangent, "crop_counts": crop_counts, "group_tokens": group_tokens, "weight_qkv": weight_qkv, "rows_qkv": rows_qkv, "cols_qkv": cols_qkv, "weight_out": weight_out, "rows_out": rows_out, "cols_out": cols_out, "weight_up": weight_up, "rows_up": rows_up, "cols_up": cols_up, "weight_down": weight_down, "rows_down": rows_down, "cols_down": cols_down, "vectors": vectors, "moment_vec": moment_vec}


EPS_NORM = 1e-06
EPS_SQUARE = 1e-30
EPS_WEIGHT = 1e-06
RATE = 0.4
padding_label = 1000000
MASKED = -1e+30
HIGHEST = lax.Precision.HIGHEST

@jax.custom_vjp
def low(v):
    return lax.optimization_barrier(v.astype(jnp.bfloat16)).astype(jnp.float32)

@jax.custom_vjp
def low_back(v):
    return v

def low_keep(v):
    return (low(v), None)

def low_pass(kept, grad):
    return (grad,)

def back_keep(v):
    return (v, None)

def back_low(kept, grad):
    return (low(grad),)
low.defvjp(low_keep, low_pass)
low_back.defvjp(back_keep, back_low)

def norm_forward(values, gain, shift):
    mean = lax.optimization_barrier(jnp.mean(values, axis=-1, keepdims=True))
    centred = values - mean
    variance = lax.optimization_barrier(jnp.mean(centred * centred, axis=-1, keepdims=True))
    return centred * lax.rsqrt(variance + EPS_NORM) * gain + shift

def segment_ids(counts, group, rows):
    first_len = jnp.where(group == 0, GLOBAL_LEN, IMAGE_LEN).astype(jnp.int32)
    first_count = counts[0].astype(jnp.int32)
    second_count = counts[1].astype(jnp.int32)
    position = jnp.arange(rows, dtype=jnp.int32)
    first_end = first_len * first_count
    second_end = first_end + LOCAL_LEN * second_count
    later = first_count + (position - first_end) // LOCAL_LEN
    label = jnp.where(position < first_end, position // first_len, jnp.where(position < second_end, later, padding_label))
    return label.astype(jnp.int32)

def device_segments(counts, group):

    def one_device(cell_counts):
        return segment_ids(cell_counts, group, TOK_DEV)
    return jax.vmap(one_device)(counts)

def unpack(vectors):
    ratio = FF // D
    up_bias = vectors[:, 3:3 + ratio].T.reshape(FF)
    base = 4 + ratio
    return (vectors[:, 0], vectors[:, 1], vectors[:, 2], up_bias, vectors[:, 3 + ratio], vectors[:, base], vectors[:, base + 1], vectors[:, base + 2], vectors[:, base + 3])

def attend(pair):
    block, segment = pair
    rows = block.shape[0]
    queries = block[:, :D].reshape(rows, HEADS, HEAD)
    keys = block[:, D:2 * D].reshape(rows, HEADS, HEAD)
    values = block[:, 2 * D:].reshape(rows, HEADS, HEAD)
    raw = jnp.einsum('qhd,khd->hqk', queries, keys, precision=HIGHEST)
    scores = low_back(raw * HEAD ** (-0.5))
    allowed = segment[:, None] == segment[None, :]
    scores = jnp.where(allowed[None], scores, MASKED)
    top = lax.optimization_barrier(jnp.max(scores, axis=2, keepdims=True))
    weights = jnp.exp(scores - top)
    probs = low(weights / lax.optimization_barrier(jnp.sum(weights, axis=2, keepdims=True)))
    mixed = jnp.einsum('hqk,khd->qhd', probs, values, precision=HIGHEST)
    return mixed.reshape(rows, D)

def group_forward(tokens, segment, params):
    weight_qkv, weight_out, weight_up, weight_down, vectors = params
    weight_qkv = low(weight_qkv)
    weight_out = low(weight_out)
    weight_up = low(weight_up)
    weight_down = low(weight_down)
    query_bias, value_bias, out_bias, up_bias, down_bias, gain_one, shift_one, gain_two, shift_two = unpack(low(vectors))
    normed = low(norm_forward(tokens, gain_one, shift_one))
    bias_qkv = jnp.concatenate([query_bias, jnp.zeros_like(query_bias), value_bias])
    projected = jnp.dot(normed, weight_qkv, precision=HIGHEST, preferred_element_type=jnp.float32) + bias_qkv
    projected = low_back(low(projected))
    blocks = tokens.shape[0] // TOK_DEV
    mixed = lax.map(jax.checkpoint(attend), (projected.reshape(blocks, TOK_DEV, 3 * D), segment.reshape(blocks, TOK_DEV)))
    mixed = low_back(low(mixed.reshape(-1, D)))
    branch = low_back(jnp.dot(mixed, weight_out, precision=HIGHEST, preferred_element_type=jnp.float32) + out_bias)
    middle = tokens + branch
    normed_two = low(norm_forward(middle, gain_two, shift_two))
    before = low_back(jnp.dot(normed_two, weight_up, precision=HIGHEST, preferred_element_type=jnp.float32) + up_bias)
    hidden = low(jax.nn.gelu(before, approximate=False))
    second = low_back(jnp.dot(hidden, weight_down, precision=HIGHEST, preferred_element_type=jnp.float32) + down_bias)
    return middle + second

def factored(grad, weight, rows, cols, decay):
    square = grad * grad + EPS_SQUARE
    rows_new = decay * rows + (1.0 - decay) * lax.optimization_barrier(jnp.mean(square, axis=1))
    cols_new = decay * cols + (1.0 - decay) * lax.optimization_barrier(jnp.mean(square, axis=0))
    estimate = rows_new[:, None] * cols_new[None, :] / jnp.mean(rows_new)
    scale = jnp.sqrt(jnp.mean(weight * weight) + EPS_WEIGHT)
    weight_new = weight - RATE * scale * grad * lax.rsqrt(estimate)
    return (grad, rows_new, cols_new, weight_new, weight_new.astype(jnp.bfloat16))

def reference(tokens_in, cotangent, crop_counts, group_tokens, weight_qkv, rows_qkv, cols_qkv, weight_out, rows_out, cols_out, weight_up, rows_up, cols_up, weight_down, rows_down, cols_down, vectors, moment_vec):
    cells = N_DP * N_FSDP
    group_rows = cells * TOK_DEV
    counts = crop_counts.reshape(2, cells, 2)
    segments = jnp.stack([device_segments(counts[group], group).reshape(group_rows) for group in range(2)])
    valid = (segments < padding_label).astype(jnp.float32)
    tokens = tokens_in.astype(jnp.float32).reshape(2, group_rows, D)
    grad_output = cotangent.astype(jnp.float32).reshape(2, group_rows, D) * valid[:, :, None]
    params = (weight_qkv, weight_out, weight_up, weight_down, vectors)

    def both(tokens_all, params_zero, params_one):
        return jnp.stack([group_forward(tokens_all[0], segments[0], params_zero), group_forward(tokens_all[1], segments[1], params_one)])
    output, pullback = jax.vjp(both, tokens, params, params)
    grad_tokens, grads_zero, grads_one = pullback(grad_output)
    total = (group_tokens[0] + group_tokens[1]).astype(jnp.float32)
    share_zero = group_tokens[0].astype(jnp.float32) / total
    share_one = group_tokens[1].astype(jnp.float32) / total

    def combine(first, second):
        return share_zero * first + share_one * second
    grads = jax.tree.map(combine, grads_zero, grads_one)
    decay = 1.0 - float(STEP) ** (-0.8)
    first = factored(grads[0], weight_qkv, rows_qkv, cols_qkv, decay)
    second = factored(grads[1], weight_out, rows_out, cols_out, decay)
    third = factored(grads[2], weight_up, rows_up, cols_up, decay)
    fourth = factored(grads[3], weight_down, rows_down, cols_down, decay)
    grad_vec = grads[4]
    moment_new = decay * moment_vec + (1.0 - decay) * (grad_vec * grad_vec + EPS_SQUARE)
    scale = jnp.sqrt(lax.optimization_barrier(jnp.mean(vectors * vectors, axis=0)) + EPS_WEIGHT)
    vectors_new = vectors - RATE * scale[None, :] * grad_vec * lax.rsqrt(moment_new)
    return (output.reshape(-1, D).astype(jnp.bfloat16), grad_tokens.reshape(-1, D), first[0], first[1], first[2], first[3], first[4], second[0], second[1], second[2], second[3], second[4], third[0], third[1], third[2], third[3], third[4], fourth[0], fourth[1], fourth[2], fourth[3], fourth[4], grad_vec, moment_new, vectors_new, vectors_new.astype(jnp.bfloat16))
```

```python
from functools import partial

import jax
import jax.numpy as jnp
from jax import lax
from jax.experimental import pallas as pl
from jax.experimental.pallas import tpu as pltpu
from jax.sharding import PartitionSpec as P

D = 1024
HEADS = 16
HEAD = 64
FF = 4096
GLOBAL_LEN = 50
LOCAL_LEN = 10
IMAGE_LEN = 145
STEP = 3

EPS_NORM = 1e-06
EPS_SQUARE = 1e-30
EPS_WEIGHT = 1e-06
RATE = 0.4
padding_label = 1000000
MASKED = -1e30
DECAY = 1.0 - float(STEP) ** (-0.8)

bf16 = jnp.bfloat16
f32 = jnp.float32


def norm_forward(values, gain, shift):
    mean = jnp.mean(values, axis=-1, keepdims=True)
    centred = values - mean
    variance = jnp.mean(centred * centred, axis=-1, keepdims=True)
    return centred * lax.rsqrt(variance + EPS_NORM) * gain + shift


def segment_ids(counts, group, rows):
    first_len = jnp.where(group == 0, GLOBAL_LEN, IMAGE_LEN).astype(jnp.int32)
    first_count = counts[0]
    second_count = counts[1]
    position = jnp.arange(rows, dtype=jnp.int32)
    first_end = first_len * first_count
    second_end = first_end + LOCAL_LEN * second_count
    later = first_count + (position - first_end) // LOCAL_LEN
    return jnp.where(
        position < first_end,
        position // first_len,
        jnp.where(position < second_end, later, padding_label),
    )


def unpack(vectors):
    ratio = FF // D
    up_bias = vectors[:, 3 : 3 + ratio].T.reshape(FF)
    base = 4 + ratio
    return (
        vectors[:, 0],
        vectors[:, 1],
        vectors[:, 2],
        up_bias,
        vectors[:, 3 + ratio],
        vectors[:, base],
        vectors[:, base + 1],
        vectors[:, base + 2],
        vectors[:, base + 3],
    )


def dot(a, b):
    return jnp.dot(a, b, preferred_element_type=f32)


def dot_nt(a, b):
    return lax.dot_general(a, b, (((1,), (1,)), ((), ())), preferred_element_type=f32)


def dot_tn(a, b):
    return lax.dot_general(a, b, (((0,), (0,)), ((), ())), preferred_element_type=f32)


def head_probs(queries, keys, allowed):
    scores = dot_nt(queries, keys) * HEAD ** (-0.5)
    scores = jnp.where(allowed, scores, MASKED)
    weights = jnp.exp(scores - jnp.max(scores, axis=1, keepdims=True))
    return weights * (1.0 / jnp.sum(weights, axis=1, keepdims=True))


def attend_kernel(seg_col, seg_row, projected, mixed):
    allowed = seg_col[...] == seg_row[...]
    lane = lax.broadcasted_iota(jnp.int32, (projected.shape[0], 2 * HEAD), 1)
    first = lane < HEAD
    for pair in range(HEADS // 2):
        queries, keys, values = (
            projected[:, at : at + 2 * HEAD]
            for at in range(2 * HEAD * pair, 3 * D, D)
        )
        parts = []
        for mask in (first, jnp.logical_not(first)):
            probs = head_probs(jnp.where(mask, queries, 0), keys, allowed)
            parts.append(dot(probs.astype(bf16), values))
        at = 2 * HEAD * pair
        mixed[:, at : at + 2 * HEAD] = jnp.where(first, *parts).astype(bf16)


def attend_back_kernel(seg_col, seg_row, projected, grad_mixed, grad):
    allowed = seg_col[...] == seg_row[...]
    lane = lax.broadcasted_iota(jnp.int32, (projected.shape[0], 2 * HEAD), 1)
    first = lane < HEAD
    scale = HEAD ** (-0.5)
    for pair in range(HEADS // 2):
        at = 2 * HEAD * pair
        queries, keys, values = (
            projected[:, start : start + 2 * HEAD] for start in range(at, 3 * D, D)
        )
        out = grad_mixed[:, at : at + 2 * HEAD]
        parts = []
        for mask in (first, jnp.logical_not(first)):
            probs = head_probs(jnp.where(mask, queries, 0), keys, allowed)
            grad_probs = dot_nt(jnp.where(mask, out, 0), values)
            inner = jnp.sum(probs * grad_probs, axis=1, keepdims=True)
            grad_scores = (probs * (grad_probs - inner)).astype(bf16)
            parts.append(
                (
                    dot(grad_scores, keys) * scale,
                    dot_tn(grad_scores, queries) * scale,
                    dot_tn(probs.astype(bf16), out),
                )
            )
        for index in range(3):
            both = jnp.where(first, parts[0][index], parts[1][index])
            grad[:, index * D + at : index * D + at + 2 * HEAD] = both.astype(bf16)


def attend(segment, projected):
    shape = (projected.shape[0], D)
    values = [segment[:, None], segment[None, :], projected]
    return call("attend", attend_kernel, [(shape, bf16)], [], values, [])[0]


def attend_back(segment, projected, grad_mixed):
    values = [segment[:, None], segment[None, :], projected, grad_mixed]
    return call("attend_back", attend_back_kernel, [(projected.shape, bf16)], [], values, [])[0]


SWAP = ((0, 1), (1, 0))
BLOCK = 256
UNIT = 512


def in_hbm(value):
    return pltpu.with_memory_space_constraint(value, pltpu.HBM)


def in_vmem(value):
    return pltpu.with_memory_space_constraint(value, pltpu.VMEM)


def any_spec():
    return pl.BlockSpec(memory_space=pl.ANY)


def gelu_parts(before):
    normal = 0.5 * (1.0 + lax.erf(before * (0.5**0.5)))
    slope = normal + before * jnp.exp(-0.5 * before * before) * ((2.0 * jnp.pi) ** -0.5)
    return (before * normal).astype(bf16), slope


def forward_matmul(finish, where, act, weight, pieces, extras, out_types, deps):
    rows, own_rows = act.shape[0], weight.shape[0]
    cols = weight.shape[1]
    blocks = cols // UNIT
    share = blocks // len(pieces)
    half_rows = pieces[0][0].shape[0]
    flat = [piece for pair in pieces for piece in pair]
    count = len(extras)

    def kernel(where, act, weight, *refs):
        pairs, refs = refs[: len(flat)], refs[len(flat) :]
        outs, (squares, rest, total) = refs[count + len(deps) : -3], refs[-3:]
        step = pl.program_id(0)
        quarter = own_rows // 4
        y, first = where[0], where[1]

        @pl.when(step == 0)
        def _():
            for k in range(4):
                at = pl.multiple_of((1 - y) * own_rows + (first ^ k) * quarter, 128)
                rest[:, k * quarter : (k + 1) * quarter] = act[:, pl.ds(at, quarter)]

        value = weight[...]
        squares[...] = jnp.sum((value * value).reshape(-1, 8, value.shape[1]), axis=0)
        own = act[:, pl.ds(pl.multiple_of(y * own_rows, 128), own_rows)]
        total[...] = dot(own, value.astype(bf16))
        for index in range(len(pieces)):

            @pl.when(step // share == index)
            def _(index=index):
                total[...] += dot(rest[:, :half_rows], pairs[2 * index][...])
                total[...] += dot(rest[:, half_rows:], pairs[2 * index + 1][...])

        finish(total[...], refs[:count], outs)

    def piece_spec(index):
        return pl.BlockSpec(
            (half_rows, UNIT), lambda g, s: (0, jnp.clip(g - index * share, 0, share - 1))
        )

    return pl.pallas_call(
        kernel,
        grid_spec=pltpu.PrefetchScalarGridSpec(
            num_scalar_prefetch=1,
            grid=(blocks,),
            in_specs=[
                pl.BlockSpec(act.shape, lambda g, s: (0, 0)),
                pl.BlockSpec((own_rows, UNIT), lambda g, s: (0, g)),
            ]
            + [piece_spec(index // 2) for index in range(len(flat))]
            + [pl.BlockSpec((extra.shape[0], UNIT), lambda g, s: (0, g)) for extra in extras]
            + [any_spec()] * len(deps),
            out_specs=[pl.BlockSpec((rows, UNIT), lambda g, s: (0, g))] * len(out_types)
            + [pl.BlockSpec((8, UNIT), lambda g, s: (0, g))],
            scratch_shapes=[pltpu.VMEM((rows, own_rows), bf16), pltpu.VMEM((rows, UNIT), f32)],
        ),
        out_shape=[
            (pltpu.HBM if streamed else jax.ShapeDtypeStruct)((rows, cols), dtype)
            for dtype, streamed in out_types
        ]
        + [jax.ShapeDtypeStruct((8, cols), f32)],
        compiler_params=pltpu.CompilerParams(vmem_limit_bytes=20 << 20),
        name="forward_matmul",
    )(where, act, weight, *flat, *extras, *deps)


def backward_matmul(where, grad, weight, pieces, dtype, deps):
    rows, own_rows = grad.shape[0], weight.shape[0]
    blocks = weight.shape[1] // UNIT
    share = blocks // len(pieces)
    half_rows = pieces[0][0].shape[0]
    flat = [piece for pair in pieces for piece in pair]

    def kernel(where, grad, weight, *refs):
        pairs = refs[: len(flat)]
        out, own, rest = refs[-3:]
        step = pl.program_id(0)
        quarter = own_rows // 4
        y, first = where[0], where[1]

        @pl.when(step == 0)
        def _():
            own[...] = jnp.zeros_like(own)
            rest[...] = jnp.zeros_like(rest)

        own[...] += dot_nt(grad[...], weight[...].astype(bf16))
        for index in range(len(pieces)):

            @pl.when(step // share == index)
            def _(index=index):
                rest[:, :half_rows] += dot_nt(grad[...], pairs[2 * index][...])
                rest[:, half_rows:] += dot_nt(grad[...], pairs[2 * index + 1][...])

        @pl.when(step == blocks - 1)
        def _():
            out[:, pl.ds(pl.multiple_of(y * own_rows, 128), own_rows)] = own[...].astype(dtype)
            for k in range(4):
                at = pl.multiple_of((1 - y) * own_rows + (first ^ k) * quarter, 128)
                part = rest[:, k * quarter : (k + 1) * quarter]
                out[:, pl.ds(at, quarter)] = part.astype(dtype)

    def piece_spec(index):
        return pl.BlockSpec(
            (half_rows, UNIT), lambda g, s: (0, jnp.clip(g - index * share, 0, share - 1))
        )

    return pl.pallas_call(
        kernel,
        grid_spec=pltpu.PrefetchScalarGridSpec(
            num_scalar_prefetch=1,
            grid=(blocks,),
            in_specs=[
                pl.BlockSpec((rows, UNIT), lambda g, s: (0, g)),
                pl.BlockSpec((own_rows, UNIT), lambda g, s: (0, g)),
            ]
            + [piece_spec(index // 2) for index in range(len(flat))]
            + [any_spec()] * len(deps),
            out_specs=pl.BlockSpec((rows, 2 * own_rows), lambda g, s: (0, 0)),
            scratch_shapes=[pltpu.VMEM((rows, own_rows), f32)] * 2,
        ),
        out_shape=jax.ShapeDtypeStruct((rows, 2 * own_rows), dtype),
        compiler_params=pltpu.CompilerParams(vmem_limit_bytes=14 << 20),
        name="backward_matmul",
    )(where, grad, weight, *flat, *deps)


def slope_matmul(where, grad, weight, pieces, slope, deps):
    rows, own_rows = grad.shape[0], weight.shape[0]
    quarter = own_rows // 4

    def kernel(where, grad, weight, half, other, slope, *refs):
        out = refs[-1]
        step = pl.program_id(0)

        @pl.when(step < 4)
        def _():
            out[...] = (dot_nt(grad[...], weight[...].astype(bf16)) * slope[...]).astype(bf16)

        for low, piece in ((4, half), (6, other)):

            @pl.when(jnp.logical_and(step >= low, step < low + 2))
            def _(piece=piece):
                out[...] = (dot_nt(grad[...], piece[...]) * slope[...]).astype(bf16)

    def place(g, s):
        return (0, jnp.where(g < 4, s[0] * 4 + g, (1 - s[0]) * 4 + (s[1] ^ jnp.maximum(g - 4, 0))))

    def piece_spec(low):
        return pl.BlockSpec((quarter, D), lambda g, s: (jnp.clip(g - low, 0, 1), 0))

    return pl.pallas_call(
        kernel,
        grid_spec=pltpu.PrefetchScalarGridSpec(
            num_scalar_prefetch=1,
            grid=(8,),
            in_specs=[
                pl.BlockSpec(grad.shape, lambda g, s: (0, 0)),
                pl.BlockSpec((quarter, D), lambda g, s: (jnp.minimum(g, 3), 0)),
                piece_spec(4),
                piece_spec(6),
                pl.BlockSpec((rows, quarter), place),
            ]
            + [any_spec()] * len(deps),
            out_specs=pl.BlockSpec((rows, quarter), place),
        ),
        out_shape=jax.ShapeDtypeStruct((rows, 2 * own_rows), bf16),
        compiler_params=pltpu.CompilerParams(vmem_limit_bytes=14 << 20),
        name="slope_matmul",
    )(where, grad, weight, *pieces, in_hbm(slope), *deps)


def finish_kernel(where, mine, theirs, *refs):
    grad, sums = refs[-2:]

    @pl.when(pl.program_id(0) == 0)
    def _():
        sums[...] = jnp.zeros_like(sums)

    mine, theirs = mine[...].astype(f32), theirs[...].astype(f32)

    @pl.when(where[0] == 0)
    def _():
        grad[:, :UNIT] = mine
        grad[:, UNIT:] = theirs

    @pl.when(where[0] == 1)
    def _():
        grad[:, :UNIT] = theirs
        grad[:, UNIT:] = mine

    mine, theirs = mine * mine, theirs * theirs
    sums[0:1] += jnp.sum(mine, axis=0, keepdims=True)
    sums[1:2] += jnp.sum(theirs, axis=0, keepdims=True)
    both = mine + theirs
    high = both.astype(bf16)
    low = (both - high.astype(f32)).astype(bf16)
    ones = jnp.ones((8, UNIT), bf16)
    rows = dot_nt(ones, high) + dot_nt(ones, low)
    for step in range(UNIT // BLOCK):

        @pl.when(pl.program_id(0) == step)
        def _(step=step):
            sums[2:3, step * BLOCK : (step + 1) * BLOCK] = rows[:1]


def finish(by_rows, index, mine, theirs, at, shape, grad, core):
    if by_rows:
        place = lambda g, s: (2 * index + g, 0)
    else:
        place = lambda g, s: (g, index)
    piece = pl.BlockSpec((BLOCK, UNIT), lambda g, s: (2 * at + g, 0))
    extra = [] if grad is None else [in_hbm(grad)]
    return pl.pallas_call(
        finish_kernel,
        grid_spec=pltpu.PrefetchScalarGridSpec(
            num_scalar_prefetch=1,
            grid=(UNIT // BLOCK,),
            in_specs=[piece, piece] + [any_spec()] * len(extra),
            out_specs=[
                pl.BlockSpec((BLOCK, 2 * UNIT), place),
                pl.BlockSpec((8, UNIT), lambda g, s: (0, 0)),
            ],
        ),
        out_shape=[pltpu.HBM(shape, f32), jax.ShapeDtypeStruct((8, UNIT), f32)],
        input_output_aliases={3: 0} if extra else {},
        compiler_params=pltpu.CompilerParams(vmem_limit_bytes=10 << 20),
        cost_estimate=pl.CostEstimate(flops=1, bytes_accessed=1, transcendentals=0),
        name="finish",
    )(core.reshape(1), mine, theirs, *extra)


def update_kernel(units, where, *refs):
    pieces = refs[: 2 * units]
    weight, row_factor, col_factor = refs[2 * units : 2 * units + 3]
    weight_new, weight_half = refs[-2:]
    unit = pl.program_id(0) // 2
    for index in range(units):
        for core in range(2):

            @pl.when(jnp.logical_and(unit == index, where[0] == core))
            def _(index=index, core=core):
                sides = pieces[2 * index : 2 * index + 2]
                for side in range(2):
                    at = slice(side * UNIT, (side + 1) * UNIT)
                    grad = sides[side ^ core][...].astype(f32)
                    new = weight[:, at] - grad * (row_factor[...] * col_factor[:, at])
                    weight_new[:, at] = new
                    weight_half[:, at] = new.astype(bf16)


def update(by_rows, pieces, weight, row_factor, col_factor, core):
    units = len(pieces)
    if by_rows:
        place = lambda g, s: (g, 0)
        row_place = lambda g, s: (g, 0)
        col_place = lambda g, s: (0, 0)
    else:
        place = lambda g, s: (g % 2, g // 2)
        row_place = lambda g, s: (g % 2, 0)
        col_place = lambda g, s: (0, g // 2)

    def piece_spec(index, at):
        return pl.BlockSpec(
            (BLOCK, UNIT), lambda g, s: (2 * at + jnp.clip(g - 2 * index, 0, 1), 0)
        )

    specs, values = [], []
    for index, (mine, theirs, at) in enumerate(pieces):
        specs += [piece_spec(index, at)] * 2
        values += [in_hbm(mine), in_hbm(theirs)]
    block = pl.BlockSpec((BLOCK, 2 * UNIT), place)
    shape = weight.shape
    return pl.pallas_call(
        partial(update_kernel, units),
        grid_spec=pltpu.PrefetchScalarGridSpec(
            num_scalar_prefetch=1,
            grid=(2 * units,),
            in_specs=specs
            + [
                block,
                pl.BlockSpec((BLOCK, 1), row_place),
                pl.BlockSpec((1, 2 * UNIT), col_place),
            ],
            out_specs=[block, block],
        ),
        out_shape=[pltpu.HBM(shape, f32), pltpu.HBM(shape, bf16)],
        compiler_params=pltpu.CompilerParams(vmem_limit_bytes=14 << 20),
        name="update",
    )(core.reshape(1), *values, weight, row_factor, col_factor)


def swap_by(first, axis, mine, theirs):
    return jnp.concatenate(
        [jnp.where(first, mine, theirs), jnp.where(first, theirs, mine)], axis=axis
    )


def call(name, kernel, out_shapes, smem, inputs, deps, held=False):
    place = pltpu.VMEM if held else jax.ShapeDtypeStruct
    if held:
        inputs = [in_vmem(value) for value in inputs]
    count = len(smem) + len(inputs)

    def body(*refs):
        kernel(*refs[:count], *refs[count + len(deps) :])

    return pl.pallas_call(
        body,
        in_specs=[pl.BlockSpec(memory_space=pltpu.SMEM)] * len(smem)
        + [pl.BlockSpec(memory_space=pltpu.VMEM)] * len(inputs)
        + [any_spec()] * len(deps),
        out_specs=[pl.BlockSpec(memory_space=pltpu.VMEM)] * len(out_shapes),
        out_shape=[place(shape, dtype) for shape, dtype in out_shapes],
        compiler_params=pltpu.CompilerParams(vmem_limit_bytes=24 << 20),
        cost_estimate=pl.CostEstimate(flops=1, bytes_accessed=1, transcendentals=0),
        name=name,
    )(*smem, *inputs, *deps)


def ordered(name, values, shape, deps):
    def kernel(*refs):
        out = refs[-1]
        at = 0
        for ref in refs[:-1]:
            rows = ref.shape[0]
            out[at : at + rows] = ref[...].astype(bf16)
            at += rows

    return call(name, kernel, [(shape, bf16)], [], values, deps)[0]


class Unit:
    pass


class Torus:
    x_pairs = tuple((i, i ^ 1) for i in range(8))
    z_in = tuple((z * 2 + x, w * 2 + x) for x in range(2) for z, w in ((0, 1), (3, 2)))
    z_mid = tuple((z * 2 + x, w * 2 + x) for x in range(2) for z, w in ((1, 2), (2, 1)))
    z_out = tuple((z * 2 + x, w * 2 + x) for x in range(2) for z, w in ((1, 0), (2, 3)))
    z_swap = z_in + z_out
    planes = [[z * 2, z * 2 + 1, 8 + z * 2, 8 + z * 2 + 1] for z in range(4)]
    sizes = (2, 2, 2, 2, 2, 1, 1)

    def __init__(self, share):
        self.core = lax.axis_index("res")
        place = lax.axis_index("dp")
        self.x = place % 2
        self.z = place // 2
        self.y = lax.axis_index("fsdp")
        self.inner = jnp.logical_or(self.z == 1, self.z == 2)
        self.share = share
        self.share_in = share.reshape(1)
        self.inner_in = self.inner.astype(jnp.int32).reshape(1)
        self.waiting = []
        self.groups = []
        self.later = []
        self.grads = {}
        self.tokens = []
        self.tick = 0
        self.buffers = {}


    def gather_vectors(self, vectors):
        own = vectors.astype(bf16).T
        other = lax.ppermute(own, "fsdp", SWAP)
        return swap_by(self.y == 0, 1, own, other).T

    def gather_all(self, weights):
        first = 2 * self.core + self.x
        self.where = jnp.stack([self.y, first])
        self.weights = [in_hbm(weight) for weight in weights]
        parts = []
        for weight, count in zip(weights, (1, 1, 2, 1)):
            rows, cols = weight.shape[0] // 4, weight.shape[1] // count
            for sub in range(count):
                parts.append(lax.dynamic_slice(weight, (first * rows, sub * cols), (rows, cols)))
        self.from_y = []
        before = []
        for index, part in enumerate(parts):
            if index == 4:
                before = before + [self.from_y[0]]
            part = ordered("cast", [part], part.shape, before)
            before = [part]
            self.from_y.append(lax.ppermute(part, "fsdp", SWAP))
        self.from_x = {0: lax.ppermute(self.from_y[0], "dp", self.x_pairs)}
        self.pieces = {}
        self.squares = {}
        self.to_core(0, before)
        self.to_x(1, [self.from_x[0]])
        self.to_x(2, [self.from_x[0]])
        self.to_x(3, [self.pieces[0][1]])

    def to_x(self, part, after):
        piece = ordered("x_part", [self.from_y[part]], self.from_y[part].shape, after)
        self.from_x[part] = lax.ppermute(piece, "dp", self.x_pairs)

    def to_core(self, part, after):
        piece, from_x = self.from_y[part], self.from_x[part]
        rows, cols = piece.shape
        half = ordered("core_part", [piece, from_x], (2 * rows, cols), after)
        self.pieces[part] = (half, lax.ppermute(half, "res", SWAP))

    def project(self, normed, bias):
        def finish(total, extra, outs):
            outs[0][...] = (total + extra[0][...]).astype(bf16)

        projected, self.squares[0] = forward_matmul(
            finish, self.where, normed, self.weights[0], [self.pieces[0]], [bias[None]], [(bf16, False)], []
        )
        self.to_core(1, [projected])
        return projected

    def attend_out(self, mixed, tokens, bias):
        self.to_core(2, [mixed])
        self.to_core(3, [mixed, self.pieces[2][0]])
        self.to_x(4, [mixed])

        def finish(total, extra, outs):
            outs[0][...] = extra[0][...] + (total + extra[1][...])

        middle, self.squares[1] = forward_matmul(
            finish,
            self.where,
            mixed,
            self.weights[1],
            [self.pieces[1]],
            [tokens, bias[None]],
            [(f32, False)],
            [],
        )
        return middle

    def feed_up(self, normed, bias):
        def finish(total, extra, outs):
            outs[0][...], outs[1][...] = gelu_parts(total + extra[0][...])

        pieces = [self.pieces[2], self.pieces[3]]
        hidden, slope, self.squares[2] = forward_matmul(
            finish, self.where, normed, self.weights[2], pieces, [bias[None]], [(bf16, False), (f32, True)], []
        )
        self.to_core(4, [hidden])
        return hidden, slope

    def feed_down(self, hidden, middle, bias):
        def finish(total, extra, outs):
            outs[0][...] = (extra[0][...] + (total + extra[1][...])).astype(bf16)

        output, self.squares[3] = forward_matmul(
            finish,
            self.where,
            hidden,
            self.weights[3],
            [self.pieces[4]],
            [middle, bias[None]],
            [(bf16, False)],
            [self.tokens[0]],
        )
        self.require(in_hbm(output), 2)
        return output

    def back_down(self, grad, slope):
        return slope_matmul(
            self.where, grad, self.weights[3], self.pieces[4], slope, [self.tokens[0]]
        )

    def back_up(self, grad):
        pieces = [self.pieces[2], self.pieces[3]]
        return backward_matmul(self.where, grad, self.weights[2], pieces, f32, [self.tokens[1]])

    def back_out(self, grad):
        return backward_matmul(
            self.where, grad, self.weights[1], [self.pieces[1]], bf16, [self.fence(2)]
        )

    def back_project(self, grad):
        return backward_matmul(
            self.where, grad, self.weights[0], [self.pieces[0]], f32, [self.fence(5)]
        )


    def after(self, value, tick):
        return value + self.tokens[tick][0, 0]

    def fence(self, tick):
        return lax.ppermute(self.tokens[tick], "res", SWAP)

    def held_out(self, value):
        return in_hbm(value)

    def require(self, value, tick):
        self.later.append((tick, value))

    def push(self, by_rows, left, right):
        half = left.shape[1] // 2
        low, high = left[:, :half], left[:, half:]
        own = jnp.where(self.y == 0, low, high)
        other = jnp.where(self.y == 0, high, low)
        count = half // UNIT if by_rows else right.shape[1] // (2 * UNIT)
        units = []
        for index in range(count):
            unit = Unit()
            unit.by_rows, unit.index, unit.matrix = by_rows, index, units
            unit.shape = (half, right.shape[1])
            if by_rows:
                at = index * UNIT
                unit.own, unit.other = own[:, at : at + UNIT], other[:, at : at + UNIT]
                cols = right
            else:
                unit.own, unit.other = own, other
                cols = right[:, index * 2 * UNIT : (index + 1) * 2 * UNIT]
            unit.kept = jnp.where(self.core == 0, cols[:, :UNIT], cols[:, UNIT:])
            unit.sent = jnp.where(self.core == 0, cols[:, UNIT:], cols[:, :UNIT])
            units.append(unit)
        for unit in units:
            self.waiting.append(unit)
            if len(self.waiting) == self.sizes[len(self.groups)]:
                self.groups.append(self.waiting)
                self.waiting = []
                self.begin(len(self.groups) - 1, self.tokens[-1:])
                if len(self.groups) > 1:
                    self.step()
        return units

    def group(self, index):
        return self.groups[index] if 0 <= index < len(self.groups) else []

    def begin(self, index, deps):
        units = self.group(index)
        values = []
        for unit in units:
            values += [unit.own, unit.other, unit.kept, unit.sent]

        def kernel(share, *refs):
            sent_out, own_out, other_out = refs[-3:]
            for k in range(len(units)):
                own, other, kept, sent = (ref[...] for ref in refs[4 * k : 4 * k + 4])
                rows = slice(k * UNIT, (k + 1) * UNIT)
                own_out[rows] = (share[0] * dot_tn(own, kept)).astype(bf16)
                other_out[rows] = (share[0] * dot_tn(other, kept)).astype(bf16)
                at = 2 * k * UNIT
                sent_out[at : at + UNIT] = (share[0] * dot_tn(own, sent)).astype(bf16)
                at += UNIT
                sent_out[at : at + UNIT] = (share[0] * dot_tn(other, sent)).astype(bf16)

        rows = len(units) * UNIT
        shapes = [((2 * rows, UNIT), bf16), ((rows, UNIT), bf16), ((rows, UNIT), bf16)]
        sent, own, other = call("k_m", kernel, shapes, [self.share_in], values, deps, True)
        self.buffers["own", index] = own
        self.buffers["other", index] = other
        self.buffers["from_core", index] = lax.ppermute(sent, "res", SWAP)

    def step(self):
        tick = self.tick
        buffers = self.buffers
        sizes = [len(self.group(tick - k)) for k in range(6)]
        size_y, size_x, size_a, size_b, size_c, size_d = sizes
        both = max(size_a, size_c)
        names, values, out_rows = [], [], []

        def give(name, key, index):
            names.append(name)
            values.append(buffers[key, index])

        if size_y:
            give("y_kept", "other", tick)
            give("y_core", "from_core", tick)
            out_rows.append(("for_y", size_y))
        if size_x:
            give("x_kept", "own", tick - 1)
            give("x_core", "from_core", tick - 1)
            give("x_y", "from_y", tick - 1)
            out_rows.append(("for_x", size_x))
        if size_a:
            give("a_kept", "for_x", tick - 1)
            give("a_new", "from_x", tick - 1)
            out_rows.append(("v1", size_a))
        if size_b:
            give("b_kept", "v1", tick - 1)
            give("swapped", "from_swap", tick - 1)
            out_rows.append(("v2", size_b))
        if size_c:
            give("c_kept", "v2", tick - 1)
            give("c_new", "from_mid", tick - 1)
            out_rows.append(("v3", size_c))
        if both:
            out_rows.append(("swap", both))
        if size_d:
            give("d_kept", "v3", tick - 1)
            if not size_b:
                give("swapped", "from_swap", tick - 1)
            out_rows.append(("final", size_d))
        out_names = [name for name, _ in out_rows] + ["token"]

        def kernel(inner, *refs):
            ins = dict(zip(names, refs))
            outs = dict(zip(out_names, refs[len(names) :]))
            outs["token"][...] = jnp.zeros_like(outs["token"])
            for k in range(size_y):
                rows = slice(k * UNIT, (k + 1) * UNIT)
                at = (2 * k + 1) * UNIT
                outs["for_y"][rows] = ins["y_kept"][rows] + ins["y_core"][at : at + UNIT]
            for k in range(size_x):
                rows = slice(k * UNIT, (k + 1) * UNIT)
                at = 2 * k * UNIT
                total = ins["x_kept"][rows].astype(f32) + ins["x_core"][at : at + UNIT].astype(f32)
                outs["for_x"][rows] = (total + ins["x_y"][rows].astype(f32)).astype(bf16)

            def add(kept, new, out, size):
                rows = slice(0, size * UNIT)
                outs[out][...] = ins[kept][rows] + ins[new][rows]

            if size_a:
                add("a_kept", "a_new", "v1", size_a)

                @pl.when(inner[0] == 0)
                def _():
                    outs["swap"][: size_a * UNIT] = outs["v1"][...]

            if size_b:
                add("b_kept", "swapped", "v2", size_b)
            if size_c:
                add("c_kept", "c_new", "v3", size_c)

                @pl.when(inner[0] == 1)
                def _():
                    outs["swap"][: size_c * UNIT] = outs["v3"][...]

            if size_d:

                @pl.when(inner[0] == 1)
                def _():
                    outs["final"][...] = ins["d_kept"][...]

                @pl.when(inner[0] == 0)
                def _():
                    outs["final"][...] = ins["swapped"][: size_d * UNIT]

        shapes = [((rows * UNIT, UNIT), bf16) for _, rows in out_rows] + [((8, 128), f32)]
        deps = self.tokens[-1:]
        deps += [value for when, value in self.later if when == tick]
        outs = dict(zip(out_names, call("t", kernel, shapes, [self.inner_in], values, deps, True)))
        self.tokens.append(outs["token"])
        for name in ("for_x", "v1", "v2", "v3"):
            if name in outs:
                buffers[name, tick] = outs[name]
        if size_y:
            buffers["from_y", tick] = lax.ppermute(outs["for_y"], "fsdp", SWAP)
        if size_x:
            buffers["from_x", tick] = lax.ppermute(outs["for_x"], "dp", self.x_pairs)
        if both:
            buffers["from_swap", tick] = lax.ppermute(outs["swap"], "dp", self.z_swap)
        if size_b:
            buffers["from_mid", tick] = lax.ppermute(outs["v2"], "dp", self.z_mid)
        if size_d:
            final = outs["final"]
            received = lax.ppermute(final, "res", SWAP)
            ended = self.group(tick - 5)
            for k, unit in enumerate(ended):
                unit.piece = (final, received, k)
                grad = self.grads.get(id(unit.matrix))
                grad, sums = finish(
                    unit.by_rows, unit.index, final, received, k, unit.shape, grad, self.core
                )
                self.grads[id(unit.matrix)] = grad
                unit.cols, unit.rows = (sums[0], sums[1]), sums[2]
                self.later.append((tick + 2, sums))
        self.tick += 1

    def update(self, by_rows, units, weight, rows, cols, index):
        pieces = [unit.piece for unit in units]
        row_sums = [unit.rows for unit in units]
        col_sums = [swap_by(self.core == 0, 0, *unit.cols) for unit in units]
        square_total = jnp.sum(self.squares[index])
        full_rows = 2 * weight.shape[0]
        row_sum = jnp.concatenate(row_sums) if by_rows else sum(row_sums)
        col_sum = sum(col_sums) if by_rows else jnp.concatenate(col_sums)
        rows_new = DECAY * rows + (1.0 - DECAY) * (row_sum / weight.shape[1] + EPS_SQUARE)
        both = jnp.concatenate([col_sum, jnp.stack([jnp.sum(rows_new), square_total])])
        both = both + lax.ppermute(both, "fsdp", SWAP)
        cols_new = DECAY * cols + (1.0 - DECAY) * (both[:-2] / full_rows + EPS_SQUARE)
        row_mean = both[-2] / full_rows
        scale = jnp.sqrt(both[-1] / (full_rows * weight.shape[1]) + EPS_WEIGHT)
        row_factor = RATE * scale * lax.rsqrt(rows_new / row_mean)
        col_factor = lax.rsqrt(cols_new)
        new, half = update(
            by_rows, pieces, in_hbm(weight), row_factor[:, None], col_factor[None, :], self.core
        )
        grad = self.grads[id(units)]
        return [grad, rows_new, cols_new, new, half]

    def vectors_step(self):
        step, value = self.vectors
        deps = self.tokens[-1:]

        def total(kernel, values, shape):
            return call("vectors", kernel, [(shape, f32)], [], values, deps)[0]

        def add(mine, theirs, out):
            out[...] = mine[...] + theirs[...]

        if step > 0:
            kept, received = value
            if step == 6:
                return jnp.where(self.inner, kept, received)
            value = total(add, [kept, received], kept.shape)
        else:
            value = total(lambda mine, out: out.__setitem__(..., mine[...]), [value], value.shape)
        kept = sent = value
        if step == 1:
            half = value.shape[1] // 2
            low, high = value[:, :half], value[:, half:]
            kept = jnp.where(self.y == 0, low, high)
            sent = jnp.where(self.y == 0, high, low)
        axis = ("res", "fsdp", "dp", "dp", "dp", "dp")[step]
        pairs = (SWAP, SWAP, self.x_pairs, self.z_in, self.z_mid, self.z_out)[step]
        received = lax.ppermute(sent, axis, pairs)
        self.require(received, self.tick)
        self.vectors = (step + 1, (kept, received))

    def begin_vectors(self, grad):
        self.vectors = (0, grad)

    def pair_sum(self, value):
        return value + lax.ppermute(value, "fsdp", SWAP)


class AnyMesh:
    def __init__(self, share):
        self.share = share

    def after(self, value, tick):
        return value

    def gather_vectors(self, vectors):
        return lax.all_gather(vectors.astype(bf16), "fsdp", axis=0, tiled=True)

    def gather_all(self, weights):
        self.weights = [self.gather_vectors(weight) for weight in weights]

    def project(self, normed, bias):
        return (dot(normed, self.weights[0]) + bias).astype(bf16)

    def attend_out(self, mixed, tokens, bias):
        return tokens + (dot(mixed, self.weights[1]) + bias)

    def feed_up(self, normed, bias):
        return gelu_parts(dot(normed, self.weights[2]) + bias)

    def feed_down(self, hidden, middle, bias):
        return (middle + (dot(hidden, self.weights[3]) + bias)).astype(bf16)

    def back_down(self, grad, slope):
        return (dot_nt(grad, self.weights[3]) * slope).astype(bf16)

    def back_up(self, grad):
        return dot_nt(grad, self.weights[2])

    def back_out(self, grad):
        return dot_nt(grad, self.weights[1]).astype(bf16)

    def back_project(self, grad):
        return dot_nt(grad, self.weights[0])

    def push(self, by_rows, left, right):
        grad = self.share * dot_tn(left, right)
        grad = lax.psum_scatter(grad, "fsdp", scatter_dimension=0, tiled=True)
        return lax.psum(grad, ("res", "dp"))

    def held_out(self, value):
        return value

    def require(self, value, tick):
        pass

    def step(self):
        pass

    def begin_vectors(self, grad):
        grad = lax.psum_scatter(grad, "fsdp", scatter_dimension=1, tiled=True)
        self.vectors = lax.psum(grad, ("res", "dp"))

    def vectors_step(self):
        return self.vectors

    def pair_sum(self, value):
        return lax.psum(value, "fsdp")

    def update(self, by_rows, grad, weight, rows, cols, index):
        square_total = jnp.sum(weight * weight)
        full_rows = weight.shape[0] * lax.axis_size("fsdp")
        square = grad * grad + EPS_SQUARE
        rows_new = DECAY * rows + (1.0 - DECAY) * jnp.mean(square, axis=1)
        col_sum, row_total, weight_total = self.pair_sum(
            (jnp.sum(square, axis=0), jnp.sum(rows_new), square_total)
        )
        cols_new = DECAY * cols + (1.0 - DECAY) * col_sum / full_rows
        row_mean = row_total / full_rows
        scale = jnp.sqrt(weight_total / (full_rows * weight.shape[1]) + EPS_WEIGHT)
        estimate = rows_new[:, None] * cols_new[None, :] / row_mean
        weight_new = weight - RATE * scale * grad * lax.rsqrt(estimate)
        return [grad, rows_new, cols_new, weight_new, weight_new.astype(bf16)]


def on_device(
    special,
    tokens_in,
    cotangent,
    crop_counts,
    group_tokens,
    weight_qkv,
    rows_qkv,
    cols_qkv,
    weight_out,
    rows_out,
    cols_out,
    weight_up,
    rows_up,
    cols_up,
    weight_down,
    rows_down,
    cols_down,
    vectors,
    moment_vec,
):
    group = lax.axis_index("res")
    rows = tokens_in.shape[0]
    total = (group_tokens[0] + group_tokens[1]).astype(f32)
    share = jnp.where(group == 0, group_tokens[0], group_tokens[1]).astype(f32) / total
    comm = (Torus if special else AnyMesh)(share)
    segment = segment_ids(crop_counts.reshape(2), group, rows)
    valid = (segment < padding_label).astype(f32)
    tokens = tokens_in.astype(f32)
    grad_output = cotangent.astype(f32) * valid[:, None]
    grad_second = grad_output.astype(bf16)

    vector_half = comm.gather_vectors(vectors)
    comm.gather_all((weight_qkv, weight_out, weight_up, weight_down))
    (
        query_bias,
        value_bias,
        out_bias,
        up_bias,
        down_bias,
        gain_one,
        shift_one,
        gain_two,
        shift_two,
    ) = unpack(vector_half.astype(f32))

    normed, norm_back_one = jax.vjp(norm_forward, tokens, gain_one, shift_one)
    normed = normed.astype(bf16)
    bias_qkv = jnp.concatenate([query_bias, jnp.zeros_like(query_bias), value_bias])
    projected = comm.project(normed, bias_qkv)
    mixed = attend(segment, projected)
    middle = comm.attend_out(mixed, tokens, out_bias)
    normed_two, norm_back_two = jax.vjp(norm_forward, middle, gain_two, shift_two)
    normed_two = normed_two.astype(bf16)
    hidden, slope = comm.feed_up(normed_two, up_bias)
    down_grad = comm.push(True, hidden, grad_second)
    output = comm.feed_down(hidden, middle, down_bias)

    grad_before = comm.back_down(grad_second, slope)
    up_grad = comm.push(False, normed_two, grad_before)
    grad_normed_two = comm.back_up(grad_before)
    grad_middle_part, grad_gain_two, grad_shift_two = norm_back_two(grad_normed_two)
    grad_middle = grad_output + grad_middle_part
    grad_branch = grad_middle.astype(bf16)
    grad_mixed = comm.back_out(grad_branch)
    grad_projected = attend_back(segment, projected, grad_mixed)
    qkv_grad = comm.push(False, normed, grad_projected)
    out_grad = comm.push(False, mixed, grad_branch)
    grad_normed = lax.optimization_barrier(comm.back_project(grad_projected))
    grad_tokens_part, grad_gain_one, grad_shift_one = norm_back_one(grad_normed)
    grad_tokens = grad_middle + grad_tokens_part

    def column_sum(value):
        return jnp.sum(value.astype(f32), axis=0)

    bias_qkv_grad = column_sum(grad_projected)
    vec_grad = share * jnp.concatenate(
        [
            bias_qkv_grad[None, :D],
            bias_qkv_grad[None, 2 * D :],
            column_sum(grad_branch)[None],
            column_sum(grad_before).reshape(FF // D, D),
            column_sum(grad_second)[None],
            grad_gain_one[None],
            grad_shift_one[None],
            grad_gain_two[None],
            grad_shift_two[None],
        ],
        axis=0,
    )
    comm.require(grad_tokens, 7)
    comm.begin_vectors(vec_grad)
    comm.step()
    comm.vectors_step()
    down = comm.update(True, down_grad, weight_down, rows_down, cols_down, 3)
    comm.require(comm.held_out(down[-1]), 8)
    comm.step()
    comm.vectors_step()
    comm.step()
    comm.vectors_step()
    up = comm.update(False, up_grad, weight_up, rows_up, cols_up, 2)
    comm.require(comm.held_out(up[-1]), 10)
    comm.step()
    comm.vectors_step()
    comm.step()
    comm.vectors_step()
    qkv = comm.update(False, qkv_grad, weight_qkv, rows_qkv, cols_qkv, 0)
    comm.require(comm.held_out(qkv[-1]), 11)
    comm.step()
    comm.vectors_step()
    grad_vec = comm.vectors_step().T
    moment_new = DECAY * moment_vec + (1.0 - DECAY) * (grad_vec * grad_vec + EPS_SQUARE)
    square_sum = comm.pair_sum(jnp.sum(vectors * vectors, axis=0))
    vector_scale = jnp.sqrt(square_sum / D + EPS_WEIGHT)
    vectors_new = vectors - RATE * vector_scale[None, :] * grad_vec * lax.rsqrt(moment_new)
    out = comm.update(False, out_grad, weight_out, rows_out, cols_out, 1)
    return tuple(
        [output, grad_tokens]
        + qkv
        + out
        + up
        + down
        + [grad_vec, moment_new, vectors_new, vectors_new.astype(bf16)]
    )


def solution(mesh):
    special = mesh.shape["fsdp"] == 2 and mesh.shape["dp"] == 8
    token_rows = P(("res", "dp", "fsdp"), None)
    matrix_in = (P("fsdp", None), P("fsdp"), P())
    matrix_out = (P("fsdp", None), P("fsdp"), P(), P("fsdp", None), P("fsdp", None))
    return jax.shard_map(
        partial(on_device, special),
        mesh=mesh,
        in_specs=(token_rows, token_rows, P("res", "dp", "fsdp", None), P())
        + matrix_in * 4
        + (P("fsdp", None), P("fsdp", None)),
        out_specs=(token_rows, token_rows) + matrix_out * 4 + (P("fsdp", None),) * 4,
        check_vma=False,
    )
```

```python
from functools import partial

import jax
import jax.numpy as jnp
from jax import lax
from jax.experimental import pallas as pl
from jax.experimental.pallas import tpu as pltpu
from jax.sharding import PartitionSpec as P

D = 1024
HEADS = 16
HEAD = 64
FF = 4096
GLOBAL_LEN = 50
LOCAL_LEN = 10
IMAGE_LEN = 145
STEP = 3

EPS_NORM = 1e-06
EPS_SQUARE = 1e-30
EPS_WEIGHT = 1e-06
RATE = 0.4
padding_label = 1000000
MASKED = -1e30
DECAY = 1.0 - float(STEP) ** (-0.8)

bf16 = jnp.bfloat16
f32 = jnp.float32


def norm_forward(values, gain, shift):
    mean = jnp.mean(values, axis=-1, keepdims=True)
    centred = values - mean
    variance = jnp.mean(centred * centred, axis=-1, keepdims=True)
    return centred * lax.rsqrt(variance + EPS_NORM) * gain + shift


def segment_ids(counts, group, rows):
    first_len = jnp.where(group == 0, GLOBAL_LEN, IMAGE_LEN).astype(jnp.int32)
    first_count = counts[0]
    second_count = counts[1]
    position = jnp.arange(rows, dtype=jnp.int32)
    first_end = first_len * first_count
    second_end = first_end + LOCAL_LEN * second_count
    later = first_count + (position - first_end) // LOCAL_LEN
    return jnp.where(
        position < first_end,
        position // first_len,
        jnp.where(position < second_end, later, padding_label),
    )


def unpack(vectors):
    ratio = FF // D
    up_bias = vectors[:, 3 : 3 + ratio].T.reshape(FF)
    base = 4 + ratio
    return (
        vectors[:, 0],
        vectors[:, 1],
        vectors[:, 2],
        up_bias,
        vectors[:, 3 + ratio],
        vectors[:, base],
        vectors[:, base + 1],
        vectors[:, base + 2],
        vectors[:, base + 3],
    )


def dot(a, b):
    return jnp.dot(a, b, preferred_element_type=f32)


def dot_nt(a, b):
    return lax.dot_general(a, b, (((1,), (1,)), ((), ())), preferred_element_type=f32)


def dot_tn(a, b):
    return lax.dot_general(a, b, (((0,), (0,)), ((), ())), preferred_element_type=f32)


def head_probs(queries, keys, allowed):
    scores = dot_nt(queries, keys) * HEAD ** (-0.5)
    scores = jnp.where(allowed, scores, MASKED)
    weights = jnp.exp(scores - jnp.max(scores, axis=1, keepdims=True))
    return weights * (1.0 / jnp.sum(weights, axis=1, keepdims=True))


def attend_kernel(seg_col, seg_row, projected, mixed):
    allowed = seg_col[...] == seg_row[...]
    lane = lax.broadcasted_iota(jnp.int32, (projected.shape[0], 2 * HEAD), 1)
    first = lane < HEAD
    for pair in range(HEADS // 2):
        queries, keys, values = (
            projected[:, at : at + 2 * HEAD]
            for at in range(2 * HEAD * pair, 3 * D, D)
        )
        parts = []
        for mask in (first, jnp.logical_not(first)):
            probs = head_probs(jnp.where(mask, queries, 0), keys, allowed)
            parts.append(dot(probs.astype(bf16), values))
        at = 2 * HEAD * pair
        mixed[:, at : at + 2 * HEAD] = jnp.where(first, *parts).astype(bf16)


def attend_back_kernel(seg_col, seg_row, projected, grad_mixed, grad):
    allowed = seg_col[...] == seg_row[...]
    lane = lax.broadcasted_iota(jnp.int32, (projected.shape[0], 2 * HEAD), 1)
    first = lane < HEAD
    scale = HEAD ** (-0.5)
    for pair in range(HEADS // 2):
        at = 2 * HEAD * pair
        queries, keys, values = (
            projected[:, start : start + 2 * HEAD] for start in range(at, 3 * D, D)
        )
        out = grad_mixed[:, at : at + 2 * HEAD]
        parts = []
        for mask in (first, jnp.logical_not(first)):
            probs = head_probs(jnp.where(mask, queries, 0), keys, allowed)
            grad_probs = dot_nt(jnp.where(mask, out, 0), values)
            inner = jnp.sum(probs * grad_probs, axis=1, keepdims=True)
            grad_scores = (probs * (grad_probs - inner)).astype(bf16)
            parts.append(
                (
                    dot(grad_scores, keys) * scale,
                    dot_tn(grad_scores, queries) * scale,
                    dot_tn(probs.astype(bf16), out),
                )
            )
        for index in range(3):
            both = jnp.where(first, parts[0][index], parts[1][index])
            grad[:, index * D + at : index * D + at + 2 * HEAD] = both.astype(bf16)


def attend(segment, projected):
    shape = (projected.shape[0], D)
    values = [segment[:, None], segment[None, :], projected]
    return call("attend", attend_kernel, [(shape, bf16)], [], values, [])[0]


def attend_back(segment, projected, grad_mixed):
    values = [segment[:, None], segment[None, :], projected, grad_mixed]
    return call("attend_back", attend_back_kernel, [(projected.shape, bf16)], [], values, [])[0]


SWAP = ((0, 1), (1, 0))
BLOCK = 256
UNIT = 512


def in_hbm(value):
    return pltpu.with_memory_space_constraint(value, pltpu.HBM)


def in_vmem(value):
    return pltpu.with_memory_space_constraint(value, pltpu.VMEM)


def any_spec():
    return pl.BlockSpec(memory_space=pl.ANY)


def gelu_parts(before):
    normal = 0.5 * (1.0 + lax.erf(before * (0.5**0.5)))
    slope = normal + before * jnp.exp(-0.5 * before * before) * ((2.0 * jnp.pi) ** -0.5)
    return (before * normal).astype(bf16), slope


def forward_matmul(finish, where, act, weight, pieces, extras, out_types, deps):
    rows, own_rows = act.shape[0], weight.shape[0]
    cols = weight.shape[1]
    blocks = cols // UNIT
    share = blocks // len(pieces)
    half_rows = pieces[0][0].shape[0]
    flat = [piece for pair in pieces for piece in pair]
    count = len(extras)

    def kernel(where, act, weight, *refs):
        pairs, refs = refs[: len(flat)], refs[len(flat) :]
        outs, (squares, rest, total) = refs[count + len(deps) : -3], refs[-3:]
        step = pl.program_id(0)
        quarter = own_rows // 4
        y, first = where[0], where[1]

        @pl.when(step == 0)
        def _():
            for k in range(4):
                at = pl.multiple_of((1 - y) * own_rows + (first ^ k) * quarter, 128)
                rest[:, k * quarter : (k + 1) * quarter] = act[:, pl.ds(at, quarter)]

        value = weight[...]
        squares[...] = jnp.sum((value * value).reshape(-1, 8, value.shape[1]), axis=0)
        own = act[:, pl.ds(pl.multiple_of(y * own_rows, 128), own_rows)]
        total[...] = dot(own, value.astype(bf16))
        for index in range(len(pieces)):

            @pl.when(step // share == index)
            def _(index=index):
                total[...] += dot(rest[:, :half_rows], pairs[2 * index][...])
                total[...] += dot(rest[:, half_rows:], pairs[2 * index + 1][...])

        finish(total[...], refs[:count], outs)

    def piece_spec(index):
        return pl.BlockSpec(
            (half_rows, UNIT), lambda g, s: (0, jnp.clip(g - index * share, 0, share - 1))
        )

    return pl.pallas_call(
        kernel,
        grid_spec=pltpu.PrefetchScalarGridSpec(
            num_scalar_prefetch=1,
            grid=(blocks,),
            in_specs=[
                pl.BlockSpec(act.shape, lambda g, s: (0, 0)),
                pl.BlockSpec((own_rows, UNIT), lambda g, s: (0, g)),
            ]
            + [piece_spec(index // 2) for index in range(len(flat))]
            + [pl.BlockSpec((extra.shape[0], UNIT), lambda g, s: (0, g)) for extra in extras]
            + [any_spec()] * len(deps),
            out_specs=[pl.BlockSpec((rows, UNIT), lambda g, s: (0, g))] * len(out_types)
            + [pl.BlockSpec((8, UNIT), lambda g, s: (0, g))],
            scratch_shapes=[pltpu.VMEM((rows, own_rows), bf16), pltpu.VMEM((rows, UNIT), f32)],
        ),
        out_shape=[
            (pltpu.HBM if streamed else jax.ShapeDtypeStruct)((rows, cols), dtype)
            for dtype, streamed in out_types
        ]
        + [jax.ShapeDtypeStruct((8, cols), f32)],
        compiler_params=pltpu.CompilerParams(vmem_limit_bytes=20 << 20),
        name="forward_matmul",
    )(where, act, weight, *flat, *extras, *deps)


def backward_matmul(where, grad, weight, pieces, dtype, deps):
    rows, own_rows = grad.shape[0], weight.shape[0]
    blocks = weight.shape[1] // UNIT
    share = blocks // len(pieces)
    half_rows = pieces[0][0].shape[0]
    flat = [piece for pair in pieces for piece in pair]

    def kernel(where, grad, weight, *refs):
        pairs = refs[: len(flat)]
        out, own, rest = refs[-3:]
        step = pl.program_id(0)
        quarter = own_rows // 4
        y, first = where[0], where[1]

        @pl.when(step == 0)
        def _():
            own[...] = jnp.zeros_like(own)
            rest[...] = jnp.zeros_like(rest)

        own[...] += dot_nt(grad[...], weight[...].astype(bf16))
        for index in range(len(pieces)):

            @pl.when(step // share == index)
            def _(index=index):
                rest[:, :half_rows] += dot_nt(grad[...], pairs[2 * index][...])
                rest[:, half_rows:] += dot_nt(grad[...], pairs[2 * index + 1][...])

        @pl.when(step == blocks - 1)
        def _():
            out[:, pl.ds(pl.multiple_of(y * own_rows, 128), own_rows)] = own[...].astype(dtype)
            for k in range(4):
                at = pl.multiple_of((1 - y) * own_rows + (first ^ k) * quarter, 128)
                part = rest[:, k * quarter : (k + 1) * quarter]
                out[:, pl.ds(at, quarter)] = part.astype(dtype)

    def piece_spec(index):
        return pl.BlockSpec(
            (half_rows, UNIT), lambda g, s: (0, jnp.clip(g - index * share, 0, share - 1))
        )

    return pl.pallas_call(
        kernel,
        grid_spec=pltpu.PrefetchScalarGridSpec(
            num_scalar_prefetch=1,
            grid=(blocks,),
            in_specs=[
                pl.BlockSpec((rows, UNIT), lambda g, s: (0, g)),
                pl.BlockSpec((own_rows, UNIT), lambda g, s: (0, g)),
            ]
            + [piece_spec(index // 2) for index in range(len(flat))]
            + [any_spec()] * len(deps),
            out_specs=pl.BlockSpec((rows, 2 * own_rows), lambda g, s: (0, 0)),
            scratch_shapes=[pltpu.VMEM((rows, own_rows), f32)] * 2,
        ),
        out_shape=jax.ShapeDtypeStruct((rows, 2 * own_rows), dtype),
        compiler_params=pltpu.CompilerParams(vmem_limit_bytes=14 << 20),
        name="backward_matmul",
    )(where, grad, weight, *flat, *deps)


def slope_matmul(where, grad, weight, pieces, slope, deps):
    rows, own_rows = grad.shape[0], weight.shape[0]
    quarter = own_rows // 4

    def kernel(where, grad, weight, half, other, slope, *refs):
        out = refs[-1]
        step = pl.program_id(0)

        @pl.when(step < 4)
        def _():
            out[...] = (dot_nt(grad[...], weight[...].astype(bf16)) * slope[...]).astype(bf16)

        for low, piece in ((4, half), (6, other)):

            @pl.when(jnp.logical_and(step >= low, step < low + 2))
            def _(piece=piece):
                out[...] = (dot_nt(grad[...], piece[...]) * slope[...]).astype(bf16)

    def place(g, s):
        return (0, jnp.where(g < 4, s[0] * 4 + g, (1 - s[0]) * 4 + (s[1] ^ jnp.maximum(g - 4, 0))))

    def piece_spec(low):
        return pl.BlockSpec((quarter, D), lambda g, s: (jnp.clip(g - low, 0, 1), 0))

    return pl.pallas_call(
        kernel,
        grid_spec=pltpu.PrefetchScalarGridSpec(
            num_scalar_prefetch=1,
            grid=(8,),
            in_specs=[
                pl.BlockSpec(grad.shape, lambda g, s: (0, 0)),
                pl.BlockSpec((quarter, D), lambda g, s: (jnp.minimum(g, 3), 0)),
                piece_spec(4),
                piece_spec(6),
                pl.BlockSpec((rows, quarter), place),
            ]
            + [any_spec()] * len(deps),
            out_specs=pl.BlockSpec((rows, quarter), place),
        ),
        out_shape=jax.ShapeDtypeStruct((rows, 2 * own_rows), bf16),
        compiler_params=pltpu.CompilerParams(vmem_limit_bytes=14 << 20),
        name="slope_matmul",
    )(where, grad, weight, *pieces, in_hbm(slope), *deps)


def finish_kernel(where, mine, theirs, *refs):
    grad, sums = refs[-2:]

    @pl.when(pl.program_id(0) == 0)
    def _():
        sums[...] = jnp.zeros_like(sums)

    mine, theirs = mine[...].astype(f32), theirs[...].astype(f32)

    @pl.when(where[0] == 0)
    def _():
        grad[:, :UNIT] = mine
        grad[:, UNIT:] = theirs

    @pl.when(where[0] == 1)
    def _():
        grad[:, :UNIT] = theirs
        grad[:, UNIT:] = mine

    mine, theirs = mine * mine, theirs * theirs
    sums[0:1] += jnp.sum(mine, axis=0, keepdims=True)
    sums[1:2] += jnp.sum(theirs, axis=0, keepdims=True)
    both = mine + theirs
    high = both.astype(bf16)
    low = (both - high.astype(f32)).astype(bf16)
    ones = jnp.ones((8, UNIT), bf16)
    rows = dot_nt(ones, high) + dot_nt(ones, low)
    for step in range(UNIT // BLOCK):

        @pl.when(pl.program_id(0) == step)
        def _(step=step):
            sums[2:3, step * BLOCK : (step + 1) * BLOCK] = rows[:1]


def finish(by_rows, index, mine, theirs, at, shape, grad, core):
    if by_rows:
        place = lambda g, s: (2 * index + g, 0)
    else:
        place = lambda g, s: (g, index)
    piece = pl.BlockSpec((BLOCK, UNIT), lambda g, s: (2 * at + g, 0))
    extra = [] if grad is None else [in_hbm(grad)]
    return pl.pallas_call(
        finish_kernel,
        grid_spec=pltpu.PrefetchScalarGridSpec(
            num_scalar_prefetch=1,
            grid=(UNIT // BLOCK,),
            in_specs=[piece, piece] + [any_spec()] * len(extra),
            out_specs=[
                pl.BlockSpec((BLOCK, 2 * UNIT), place),
                pl.BlockSpec((8, UNIT), lambda g, s: (0, 0)),
            ],
        ),
        out_shape=[pltpu.HBM(shape, f32), jax.ShapeDtypeStruct((8, UNIT), f32)],
        input_output_aliases={3: 0} if extra else {},
        compiler_params=pltpu.CompilerParams(vmem_limit_bytes=10 << 20),
        cost_estimate=pl.CostEstimate(flops=1, bytes_accessed=1, transcendentals=0),
        name="finish",
    )(core.reshape(1), mine, theirs, *extra)


def update_kernel(units, where, *refs):
    pieces = refs[: 2 * units]
    weight, row_factor, col_factor = refs[2 * units : 2 * units + 3]
    weight_new, weight_half = refs[-2:]
    unit = pl.program_id(0) // 2
    for index in range(units):
        for core in range(2):

            @pl.when(jnp.logical_and(unit == index, where[0] == core))
            def _(index=index, core=core):
                sides = pieces[2 * index : 2 * index + 2]
                for side in range(2):
                    at = slice(side * UNIT, (side + 1) * UNIT)
                    grad = sides[side ^ core][...].astype(f32)
                    new = weight[:, at] - grad * (row_factor[...] * col_factor[:, at])
                    weight_new[:, at] = new
                    weight_half[:, at] = new.astype(bf16)


def update(by_rows, pieces, weight, row_factor, col_factor, core):
    units = len(pieces)
    if by_rows:
        place = lambda g, s: (g, 0)
        row_place = lambda g, s: (g, 0)
        col_place = lambda g, s: (0, 0)
    else:
        place = lambda g, s: (g % 2, g // 2)
        row_place = lambda g, s: (g % 2, 0)
        col_place = lambda g, s: (0, g // 2)

    def piece_spec(index, at):
        return pl.BlockSpec(
            (BLOCK, UNIT), lambda g, s: (2 * at + jnp.clip(g - 2 * index, 0, 1), 0)
        )

    specs, values = [], []
    for index, (mine, theirs, at) in enumerate(pieces):
        specs += [piece_spec(index, at)] * 2
        values += [in_hbm(mine), in_hbm(theirs)]
    block = pl.BlockSpec((BLOCK, 2 * UNIT), place)
    shape = weight.shape
    return pl.pallas_call(
        partial(update_kernel, units),
        grid_spec=pltpu.PrefetchScalarGridSpec(
            num_scalar_prefetch=1,
            grid=(2 * units,),
            in_specs=specs
            + [
                block,
                pl.BlockSpec((BLOCK, 1), row_place),
                pl.BlockSpec((1, 2 * UNIT), col_place),
            ],
            out_specs=[block, block],
        ),
        out_shape=[pltpu.HBM(shape, f32), pltpu.HBM(shape, bf16)],
        compiler_params=pltpu.CompilerParams(vmem_limit_bytes=14 << 20),
        name="update",
    )(core.reshape(1), *values, weight, row_factor, col_factor)


def swap_by(first, axis, mine, theirs):
    return jnp.concatenate(
        [jnp.where(first, mine, theirs), jnp.where(first, theirs, mine)], axis=axis
    )


def call(name, kernel, out_shapes, smem, inputs, deps, held=False):
    place = pltpu.VMEM if held else jax.ShapeDtypeStruct
    if held:
        inputs = [in_vmem(value) for value in inputs]
    count = len(smem) + len(inputs)

    def body(*refs):
        kernel(*refs[:count], *refs[count + len(deps) :])

    return pl.pallas_call(
        body,
        in_specs=[pl.BlockSpec(memory_space=pltpu.SMEM)] * len(smem)
        + [pl.BlockSpec(memory_space=pltpu.VMEM)] * len(inputs)
        + [any_spec()] * len(deps),
        out_specs=[pl.BlockSpec(memory_space=pltpu.VMEM)] * len(out_shapes),
        out_shape=[place(shape, dtype) for shape, dtype in out_shapes],
        compiler_params=pltpu.CompilerParams(vmem_limit_bytes=24 << 20),
        cost_estimate=pl.CostEstimate(flops=1, bytes_accessed=1, transcendentals=0),
        name=name,
    )(*smem, *inputs, *deps)


def ordered(name, values, shape, deps):
    def kernel(*refs):
        out = refs[-1]
        at = 0
        for ref in refs[:-1]:
            rows = ref.shape[0]
            out[at : at + rows] = ref[...].astype(bf16)
            at += rows

    return call(name, kernel, [(shape, bf16)], [], values, deps)[0]


class Unit:
    pass


class Torus:
    x_pairs = tuple((i, i ^ 1) for i in range(8))
    z_in = tuple((z * 2 + x, w * 2 + x) for x in range(2) for z, w in ((0, 1), (3, 2)))
    z_mid = tuple((z * 2 + x, w * 2 + x) for x in range(2) for z, w in ((1, 2), (2, 1)))
    z_out = tuple((z * 2 + x, w * 2 + x) for x in range(2) for z, w in ((1, 0), (2, 3)))
    z_swap = z_in + z_out
    planes = [[z * 2, z * 2 + 1, 8 + z * 2, 8 + z * 2 + 1] for z in range(4)]
    sizes = (2, 2, 2, 2, 2, 2)

    def __init__(self, share):
        self.core = lax.axis_index("res")
        place = lax.axis_index("dp")
        self.x = place % 2
        self.z = place // 2
        self.y = lax.axis_index("fsdp")
        self.inner = jnp.logical_or(self.z == 1, self.z == 2)
        self.share = share
        self.share_in = share.reshape(1)
        self.inner_in = self.inner.astype(jnp.int32).reshape(1)
        self.waiting = []
        self.groups = []
        self.later = []
        self.grads = {}
        self.tokens = []
        self.tick = 0
        self.buffers = {}


    def gather_vectors(self, vectors):
        own = vectors.astype(bf16).T
        other = lax.ppermute(own, "fsdp", SWAP)
        return swap_by(self.y == 0, 1, own, other).T

    def gather_all(self, weights):
        first = 2 * self.core + self.x
        self.where = jnp.stack([self.y, first])
        self.weights = [in_hbm(weight) for weight in weights]
        parts = []
        for weight, count in zip(weights, (1, 1, 2, 1)):
            rows, cols = weight.shape[0] // 4, weight.shape[1] // count
            for sub in range(count):
                parts.append(lax.dynamic_slice(weight, (first * rows, sub * cols), (rows, cols)))
        self.from_y = []
        before = []
        for index, part in enumerate(parts):
            if index == 4:
                before = before + [self.from_y[0]]
            part = ordered("cast", [part], part.shape, before)
            before = [part]
            self.from_y.append(lax.ppermute(part, "fsdp", SWAP))
        self.from_x = {0: lax.ppermute(self.from_y[0], "dp", self.x_pairs)}
        self.pieces = {}
        self.squares = {}
        self.to_core(0, before)
        self.to_x(1, [self.from_x[0]])
        self.to_x(2, [self.from_x[0]])
        self.to_x(3, [self.pieces[0][1]])

    def to_x(self, part, after):
        piece = ordered("x_part", [self.from_y[part]], self.from_y[part].shape, after)
        self.from_x[part] = lax.ppermute(piece, "dp", self.x_pairs)

    def to_core(self, part, after):
        piece, from_x = self.from_y[part], self.from_x[part]
        rows, cols = piece.shape
        half = ordered("core_part", [piece, from_x], (2 * rows, cols), after)
        self.pieces[part] = (half, lax.ppermute(half, "res", SWAP))

    def project(self, normed, bias):
        def finish(total, extra, outs):
            outs[0][...] = (total + extra[0][...]).astype(bf16)

        projected, self.squares[0] = forward_matmul(
            finish, self.where, normed, self.weights[0], [self.pieces[0]], [bias[None]], [(bf16, False)], []
        )
        self.to_core(1, [projected])
        return projected

    def attend_out(self, mixed, tokens, bias):
        self.to_core(2, [mixed])
        self.to_core(3, [mixed, self.pieces[2][0]])
        self.to_x(4, [mixed])

        def finish(total, extra, outs):
            outs[0][...] = extra[0][...] + (total + extra[1][...])

        middle, self.squares[1] = forward_matmul(
            finish,
            self.where,
            mixed,
            self.weights[1],
            [self.pieces[1]],
            [tokens, bias[None]],
            [(f32, False)],
            [],
        )
        return middle

    def feed_up(self, normed, bias):
        def finish(total, extra, outs):
            outs[0][...], outs[1][...] = gelu_parts(total + extra[0][...])

        pieces = [self.pieces[2], self.pieces[3]]
        hidden, slope, self.squares[2] = forward_matmul(
            finish, self.where, normed, self.weights[2], pieces, [bias[None]], [(bf16, False), (f32, True)], []
        )
        self.to_core(4, [hidden])
        return hidden, slope

    def feed_down(self, hidden, middle, bias):
        def finish(total, extra, outs):
            outs[0][...] = (extra[0][...] + (total + extra[1][...])).astype(bf16)

        output, self.squares[3] = forward_matmul(
            finish,
            self.where,
            hidden,
            self.weights[3],
            [self.pieces[4]],
            [middle, bias[None]],
            [(bf16, False)],
            [self.tokens[0]],
        )
        self.require(in_hbm(output), 2)
        return output

    def back_down(self, grad, slope):
        return slope_matmul(
            self.where, grad, self.weights[3], self.pieces[4], slope, [self.tokens[0]]
        )

    def back_up(self, grad):
        pieces = [self.pieces[2], self.pieces[3]]
        return backward_matmul(self.where, grad, self.weights[2], pieces, f32, [self.tokens[1]])

    def back_out(self, grad):
        return backward_matmul(
            self.where, grad, self.weights[1], [self.pieces[1]], bf16, [self.fence(2)]
        )

    def back_project(self, grad):
        return backward_matmul(
            self.where, grad, self.weights[0], [self.pieces[0]], f32, [self.fence(5)]
        )


    def after(self, value, tick):
        return value + self.tokens[tick][0, 0]

    def fence(self, tick):
        return lax.ppermute(self.tokens[tick], "res", SWAP)

    def held_out(self, value):
        return in_hbm(value)

    def require(self, value, tick):
        self.later.append((tick, value))

    def push(self, by_rows, left, right):
        half = left.shape[1] // 2
        low, high = left[:, :half], left[:, half:]
        own = jnp.where(self.y == 0, low, high)
        other = jnp.where(self.y == 0, high, low)
        count = half // UNIT if by_rows else right.shape[1] // (2 * UNIT)
        units = []
        for index in range(count):
            unit = Unit()
            unit.by_rows, unit.index, unit.matrix = by_rows, index, units
            unit.shape = (half, right.shape[1])
            if by_rows:
                at = index * UNIT
                unit.own, unit.other = own[:, at : at + UNIT], other[:, at : at + UNIT]
                cols = right
            else:
                unit.own, unit.other = own, other
                cols = right[:, index * 2 * UNIT : (index + 1) * 2 * UNIT]
            unit.kept = jnp.where(self.core == 0, cols[:, :UNIT], cols[:, UNIT:])
            unit.sent = jnp.where(self.core == 0, cols[:, UNIT:], cols[:, :UNIT])
            units.append(unit)
        for unit in units:
            self.waiting.append(unit)
            if len(self.waiting) == self.sizes[len(self.groups)]:
                self.groups.append(self.waiting)
                self.waiting = []
                self.begin(len(self.groups) - 1, self.tokens[-1:])
                if len(self.groups) > 1:
                    self.step()
        return units

    def group(self, index):
        return self.groups[index] if 0 <= index < len(self.groups) else []

    def begin(self, index, deps):
        units = self.group(index)
        values = []
        for unit in units:
            values += [unit.own, unit.other, unit.kept, unit.sent]

        def kernel(share, *refs):
            sent_out, own_out, other_out = refs[-3:]
            for k in range(len(units)):
                own, other, kept, sent = (ref[...] for ref in refs[4 * k : 4 * k + 4])
                rows = slice(k * UNIT, (k + 1) * UNIT)
                own_out[rows] = (share[0] * dot_tn(own, kept)).astype(bf16)
                other_out[rows] = (share[0] * dot_tn(other, kept)).astype(bf16)
                at = 2 * k * UNIT
                sent_out[at : at + UNIT] = (share[0] * dot_tn(own, sent)).astype(bf16)
                at += UNIT
                sent_out[at : at + UNIT] = (share[0] * dot_tn(other, sent)).astype(bf16)

        rows = len(units) * UNIT
        shapes = [((2 * rows, UNIT), bf16), ((rows, UNIT), bf16), ((rows, UNIT), bf16)]
        sent, own, other = call("k_m", kernel, shapes, [self.share_in], values, deps, True)
        self.buffers["own", index] = own
        self.buffers["other", index] = other
        self.buffers["from_core", index] = lax.ppermute(sent, "res", SWAP)

    def step(self):
        tick = self.tick
        buffers = self.buffers
        sizes = [len(self.group(tick - k)) for k in range(6)]
        size_y, size_x, size_a, size_b, size_c, size_d = sizes
        both = max(size_a, size_c)
        names, values, out_rows = [], [], []

        def give(name, key, index):
            names.append(name)
            values.append(buffers[key, index])

        if size_y:
            give("y_kept", "other", tick)
            give("y_core", "from_core", tick)
            out_rows.append(("for_y", size_y))
        if size_x:
            give("x_kept", "own", tick - 1)
            give("x_core", "from_core", tick - 1)
            give("x_y", "from_y", tick - 1)
            out_rows.append(("for_x", size_x))
        if size_a:
            give("a_kept", "for_x", tick - 1)
            give("a_new", "from_x", tick - 1)
            out_rows.append(("v1", size_a))
        if size_b:
            give("b_kept", "v1", tick - 1)
            give("swapped", "from_swap", tick - 1)
            out_rows.append(("v2", size_b))
        if size_c:
            give("c_kept", "v2", tick - 1)
            give("c_new", "from_mid", tick - 1)
            out_rows.append(("v3", size_c))
        if both:
            out_rows.append(("swap", both))
        if size_d:
            give("d_kept", "v3", tick - 1)
            if not size_b:
                give("swapped", "from_swap", tick - 1)
            out_rows.append(("final", size_d))
        out_names = [name for name, _ in out_rows] + ["token"]

        def kernel(inner, *refs):
            ins = dict(zip(names, refs))
            outs = dict(zip(out_names, refs[len(names) :]))
            outs["token"][...] = jnp.zeros_like(outs["token"])
            for k in range(size_y):
                rows = slice(k * UNIT, (k + 1) * UNIT)
                at = (2 * k + 1) * UNIT
                outs["for_y"][rows] = ins["y_kept"][rows] + ins["y_core"][at : at + UNIT]
            for k in range(size_x):
                rows = slice(k * UNIT, (k + 1) * UNIT)
                at = 2 * k * UNIT
                total = ins["x_kept"][rows].astype(f32) + ins["x_core"][at : at + UNIT].astype(f32)
                outs["for_x"][rows] = (total + ins["x_y"][rows].astype(f32)).astype(bf16)

            def add(kept, new, out, size):
                rows = slice(0, size * UNIT)
                outs[out][...] = ins[kept][rows] + ins[new][rows]

            if size_a:
                add("a_kept", "a_new", "v1", size_a)

                @pl.when(inner[0] == 0)
                def _():
                    outs["swap"][: size_a * UNIT] = outs["v1"][...]

            if size_b:
                add("b_kept", "swapped", "v2", size_b)
            if size_c:
                add("c_kept", "c_new", "v3", size_c)

                @pl.when(inner[0] == 1)
                def _():
                    outs["swap"][: size_c * UNIT] = outs["v3"][...]

            if size_d:

                @pl.when(inner[0] == 1)
                def _():
                    outs["final"][...] = ins["d_kept"][...]

                @pl.when(inner[0] == 0)
                def _():
                    outs["final"][...] = ins["swapped"][: size_d * UNIT]

        shapes = [((rows * UNIT, UNIT), bf16) for _, rows in out_rows] + [((8, 128), f32)]
        deps = self.tokens[-1:]
        deps += [value for when, value in self.later if when == tick]
        outs = dict(zip(out_names, call("t", kernel, shapes, [self.inner_in], values, deps, True)))
        self.tokens.append(outs["token"])
        for name in ("for_x", "v1", "v2", "v3"):
            if name in outs:
                buffers[name, tick] = outs[name]
        if size_y:
            buffers["from_y", tick] = lax.ppermute(outs["for_y"], "fsdp", SWAP)
        if size_x:
            buffers["from_x", tick] = lax.ppermute(outs["for_x"], "dp", self.x_pairs)
        if both:
            buffers["from_swap", tick] = lax.ppermute(outs["swap"], "dp", self.z_swap)
        if size_b:
            buffers["from_mid", tick] = lax.ppermute(outs["v2"], "dp", self.z_mid)
        if size_d:
            final = outs["final"]
            received = lax.ppermute(final, "res", SWAP)
            ended = self.group(tick - 5)
            for k, unit in enumerate(ended):
                unit.piece = (final, received, k)
                grad = self.grads.get(id(unit.matrix))
                grad, sums = finish(
                    unit.by_rows, unit.index, final, received, k, unit.shape, grad, self.core
                )
                self.grads[id(unit.matrix)] = grad
                unit.cols, unit.rows = (sums[0], sums[1]), sums[2]
                self.later.append((tick + 2, sums))
        self.tick += 1

    def update(self, by_rows, units, weight, rows, cols, index):
        pieces = [unit.piece for unit in units]
        row_sums = [unit.rows for unit in units]
        col_sums = [swap_by(self.core == 0, 0, *unit.cols) for unit in units]
        square_total = jnp.sum(self.squares[index])
        full_rows = 2 * weight.shape[0]
        row_sum = jnp.concatenate(row_sums) if by_rows else sum(row_sums)
        col_sum = sum(col_sums) if by_rows else jnp.concatenate(col_sums)
        rows_new = DECAY * rows + (1.0 - DECAY) * (row_sum / weight.shape[1] + EPS_SQUARE)
        both = jnp.concatenate([col_sum, jnp.stack([jnp.sum(rows_new), square_total])])
        both = both + lax.ppermute(both, "fsdp", SWAP)
        cols_new = DECAY * cols + (1.0 - DECAY) * (both[:-2] / full_rows + EPS_SQUARE)
        row_mean = both[-2] / full_rows
        scale = jnp.sqrt(both[-1] / (full_rows * weight.shape[1]) + EPS_WEIGHT)
        row_factor = RATE * scale * lax.rsqrt(rows_new / row_mean)
        col_factor = lax.rsqrt(cols_new)
        new, half = update(
            by_rows, pieces, in_hbm(weight), row_factor[:, None], col_factor[None, :], self.core
        )
        grad = self.grads[id(units)]
        return [grad, rows_new, cols_new, new, half]

    def vectors_step(self):
        step, value = self.vectors
        deps = self.tokens[-1:]

        def total(kernel, values, shape):
            return call("vectors", kernel, [(shape, f32)], [], values, deps)[0]

        def add(mine, theirs, out):
            out[...] = mine[...] + theirs[...]

        if step > 0:
            kept, received = value
            if step == 6:
                return jnp.where(self.inner, kept, received)
            value = total(add, [kept, received], kept.shape)
        else:
            value = total(lambda mine, out: out.__setitem__(..., mine[...]), [value], value.shape)
        kept = sent = value
        if step == 1:
            half = value.shape[1] // 2
            low, high = value[:, :half], value[:, half:]
            kept = jnp.where(self.y == 0, low, high)
            sent = jnp.where(self.y == 0, high, low)
        axis = ("res", "fsdp", "dp", "dp", "dp", "dp")[step]
        pairs = (SWAP, SWAP, self.x_pairs, self.z_in, self.z_mid, self.z_out)[step]
        received = lax.ppermute(sent, axis, pairs)
        self.require(received, self.tick)
        self.vectors = (step + 1, (kept, received))

    def begin_vectors(self, grad):
        self.vectors = (0, grad)

    def pair_sum(self, value):
        return value + lax.ppermute(value, "fsdp", SWAP)


class AnyMesh:
    def __init__(self, share):
        self.share = share

    def after(self, value, tick):
        return value

    def gather_vectors(self, vectors):
        return lax.all_gather(vectors.astype(bf16), "fsdp", axis=0, tiled=True)

    def gather_all(self, weights):
        self.weights = [self.gather_vectors(weight) for weight in weights]

    def project(self, normed, bias):
        return (dot(normed, self.weights[0]) + bias).astype(bf16)

    def attend_out(self, mixed, tokens, bias):
        return tokens + (dot(mixed, self.weights[1]) + bias)

    def feed_up(self, normed, bias):
        return gelu_parts(dot(normed, self.weights[2]) + bias)

    def feed_down(self, hidden, middle, bias):
        return (middle + (dot(hidden, self.weights[3]) + bias)).astype(bf16)

    def back_down(self, grad, slope):
        return (dot_nt(grad, self.weights[3]) * slope).astype(bf16)

    def back_up(self, grad):
        return dot_nt(grad, self.weights[2])

    def back_out(self, grad):
        return dot_nt(grad, self.weights[1]).astype(bf16)

    def back_project(self, grad):
        return dot_nt(grad, self.weights[0])

    def push(self, by_rows, left, right):
        grad = self.share * dot_tn(left, right)
        grad = lax.psum_scatter(grad, "fsdp", scatter_dimension=0, tiled=True)
        return lax.psum(grad, ("res", "dp"))

    def held_out(self, value):
        return value

    def require(self, value, tick):
        pass

    def step(self):
        pass

    def begin_vectors(self, grad):
        grad = lax.psum_scatter(grad, "fsdp", scatter_dimension=1, tiled=True)
        self.vectors = lax.psum(grad, ("res", "dp"))

    def vectors_step(self):
        return self.vectors

    def pair_sum(self, value):
        return lax.psum(value, "fsdp")

    def update(self, by_rows, grad, weight, rows, cols, index):
        square_total = jnp.sum(weight * weight)
        full_rows = weight.shape[0] * lax.axis_size("fsdp")
        square = grad * grad + EPS_SQUARE
        rows_new = DECAY * rows + (1.0 - DECAY) * jnp.mean(square, axis=1)
        col_sum, row_total, weight_total = self.pair_sum(
            (jnp.sum(square, axis=0), jnp.sum(rows_new), square_total)
        )
        cols_new = DECAY * cols + (1.0 - DECAY) * col_sum / full_rows
        row_mean = row_total / full_rows
        scale = jnp.sqrt(weight_total / (full_rows * weight.shape[1]) + EPS_WEIGHT)
        estimate = rows_new[:, None] * cols_new[None, :] / row_mean
        weight_new = weight - RATE * scale * grad * lax.rsqrt(estimate)
        return [grad, rows_new, cols_new, weight_new, weight_new.astype(bf16)]


def on_device(
    special,
    tokens_in,
    cotangent,
    crop_counts,
    group_tokens,
    weight_qkv,
    rows_qkv,
    cols_qkv,
    weight_out,
    rows_out,
    cols_out,
    weight_up,
    rows_up,
    cols_up,
    weight_down,
    rows_down,
    cols_down,
    vectors,
    moment_vec,
):
    group = lax.axis_index("res")
    rows = tokens_in.shape[0]
    total = (group_tokens[0] + group_tokens[1]).astype(f32)
    share = jnp.where(group == 0, group_tokens[0], group_tokens[1]).astype(f32) / total
    comm = (Torus if special else AnyMesh)(share)
    segment = segment_ids(crop_counts.reshape(2), group, rows)
    valid = (segment < padding_label).astype(f32)
    tokens = tokens_in.astype(f32)
    grad_output = cotangent.astype(f32) * valid[:, None]
    grad_second = grad_output.astype(bf16)

    vector_half = comm.gather_vectors(vectors)
    comm.gather_all((weight_qkv, weight_out, weight_up, weight_down))
    (
        query_bias,
        value_bias,
        out_bias,
        up_bias,
        down_bias,
        gain_one,
        shift_one,
        gain_two,
        shift_two,
    ) = unpack(vector_half.astype(f32))

    normed, norm_back_one = jax.vjp(norm_forward, tokens, gain_one, shift_one)
    normed = normed.astype(bf16)
    bias_qkv = jnp.concatenate([query_bias, jnp.zeros_like(query_bias), value_bias])
    projected = comm.project(normed, bias_qkv)
    mixed = attend(segment, projected)
    middle = comm.attend_out(mixed, tokens, out_bias)
    normed_two, norm_back_two = jax.vjp(norm_forward, middle, gain_two, shift_two)
    normed_two = normed_two.astype(bf16)
    hidden, slope = comm.feed_up(normed_two, up_bias)
    down_grad = comm.push(True, hidden, grad_second)
    output = comm.feed_down(hidden, middle, down_bias)

    grad_before = comm.back_down(grad_second, slope)
    up_grad = comm.push(False, normed_two, grad_before)
    grad_normed_two = comm.back_up(grad_before)
    grad_middle_part, grad_gain_two, grad_shift_two = norm_back_two(grad_normed_two)
    grad_middle = grad_output + grad_middle_part
    grad_branch = grad_middle.astype(bf16)
    grad_mixed = comm.back_out(grad_branch)
    grad_projected = attend_back(segment, projected, grad_mixed)
    qkv_grad = comm.push(False, normed, grad_projected)
    out_grad = comm.push(False, mixed, grad_branch)
    comm.step()
    grad_normed = lax.optimization_barrier(comm.back_project(grad_projected))
    grad_tokens_part, grad_gain_one, grad_shift_one = norm_back_one(grad_normed)
    grad_tokens = grad_middle + grad_tokens_part

    def column_sum(value):
        return jnp.sum(value.astype(f32), axis=0)

    bias_qkv_grad = column_sum(grad_projected)
    vec_grad = share * jnp.concatenate(
        [
            bias_qkv_grad[None, :D],
            bias_qkv_grad[None, 2 * D :],
            column_sum(grad_branch)[None],
            column_sum(grad_before).reshape(FF // D, D),
            column_sum(grad_second)[None],
            grad_gain_one[None],
            grad_shift_one[None],
            grad_gain_two[None],
            grad_shift_two[None],
        ],
        axis=0,
    )
    comm.require(grad_tokens, 7)
    comm.begin_vectors(vec_grad)
    comm.step()
    comm.vectors_step()
    down = comm.update(True, down_grad, weight_down, rows_down, cols_down, 3)
    comm.require(comm.held_out(down[-1]), 8)
    comm.step()
    comm.vectors_step()
    comm.step()
    comm.vectors_step()
    up = comm.update(False, up_grad, weight_up, rows_up, cols_up, 2)
    comm.require(comm.held_out(up[-1]), 10)
    comm.step()
    comm.vectors_step()
    comm.step()
    comm.vectors_step()
    comm.vectors_step()
    qkv = comm.update(False, qkv_grad, weight_qkv, rows_qkv, cols_qkv, 0)
    grad_vec = comm.vectors_step().T
    moment_new = DECAY * moment_vec + (1.0 - DECAY) * (grad_vec * grad_vec + EPS_SQUARE)
    square_sum = comm.pair_sum(jnp.sum(vectors * vectors, axis=0))
    vector_scale = jnp.sqrt(square_sum / D + EPS_WEIGHT)
    vectors_new = vectors - RATE * vector_scale[None, :] * grad_vec * lax.rsqrt(moment_new)
    out = comm.update(False, out_grad, weight_out, rows_out, cols_out, 1)
    return tuple(
        [output, grad_tokens]
        + qkv
        + out
        + up
        + down
        + [grad_vec, moment_new, vectors_new, vectors_new.astype(bf16)]
    )


def solution(mesh):
    special = mesh.shape["fsdp"] == 2 and mesh.shape["dp"] == 8
    token_rows = P(("res", "dp", "fsdp"), None)
    matrix_in = (P("fsdp", None), P("fsdp"), P())
    matrix_out = (P("fsdp", None), P("fsdp"), P(), P("fsdp", None), P("fsdp", None))
    return jax.shard_map(
        partial(on_device, special),
        mesh=mesh,
        in_specs=(token_rows, token_rows, P("res", "dp", "fsdp", None), P())
        + matrix_in * 4
        + (P("fsdp", None), P("fsdp", None)),
        out_specs=(token_rows, token_rows) + matrix_out * 4 + (P("fsdp", None),) * 4,
        check_vma=False,
    )
```
